256 devices in a mesh: space: 8 (over z), tm: 8 (over y, core), dir: 4 (over x).
Axes of the slice: x: 4, y: 4, z: 8, core: 2. Of those that a mesh axis runs over, the one named last changes fastest.
Arguments:
- right_side: float32 [8, 1024, 2048], P('dir', 'space', 'tm'), may hold values from -6 to 6
- spatial_basis: bfloat16 [1024, 1024], replicated, may hold values from -0.1875 to 0.1875
- temporal_basis: bfloat16 [2048, 2048], replicated, may hold values from -0.125 to 0.125
- spectral_weight: float32 [1024, 2048], P(None, ('space', 'tm')), may hold values from 0.2 to 5
- pierce_nodes: int32 [8, 16, 4, 512], P('dir', 'tm'), may hold values from 0 to 1023
- pierce_weights: float32 [8, 16, 4, 512], P('dir', 'tm'), may hold values from 0.2 to 1
Outputs:
- solution_field: float32 [8, 1024, 2048], P('dir', 'space', 'tm')
- residual: float32 [8, 1024, 2048], P('dir', 'space', 'tm')
The draws below stay inside these ranges and needn't reach their ends.
All inputs are finite; a program needn't handle non-finite values.
Results may differ from the reference program's by a relative error of at most 0.03.
Values may be sent and summed in bfloat16 or wider, within the bound.
A program may use at most 128 MiB of HBM per device.

```python
import math
import jax
import jax.numpy as jnp
from jax import lax

S = 1024
T_SIZE = 2048
STATIONS = 512
KNN = 4
TBLK = 128
ITERS = 4
DIRS = 8
NTB = 16


def with_ends(drawn, stream_key, low, top_value):
    shape = drawn.shape
    spot = [jax.random.randint(jax.random.fold_in(stream_key, axis), (), 0, shape[axis]) for axis in range(len(shape))]
    drawn = drawn.at[tuple(spot)].set(low)
    longest = shape.index(max(shape))
    spot[longest] = (spot[longest] + 1) % shape[longest]
    return drawn.at[tuple(spot)].set(top_value)


def block_levels(own_key, extent, cuts, least, largest):
    factor_of, own = 1.0, jax.random.fold_in(own_key, 6)
    for position, parts in cuts:
        heights = jnp.exp(jax.random.uniform(jax.random.fold_in(own, position), (parts,), jnp.float32, least / len(cuts), largest / len(cuts)))
        factor_of = factor_of * jnp.repeat(heights, extent[position] // parts).reshape([-1 if axis == position else 1 for axis in range(len(extent))])
    return factor_of


def bell_draw(rng, dims, deviation, bound, cuts=(), held_as=jnp.bfloat16):
    gain = block_levels(rng, dims, cuts, -0.22, 0.18) if cuts else 1.0
    drawn = jax.random.normal(rng, dims, jnp.float32) * deviation * gain
    return jnp.minimum(jnp.maximum(drawn, -bound), bound).astype(held_as)


def setup_inputs(seed: int = 0) -> dict:
    seeds = jax.random.split(jax.random.key(seed), 7)
    return {
        "right_side": bell_draw(seeds[0], (DIRS, S, T_SIZE), 1.0, 6.0, ((0, 4), (1, 8), (2, 8)), jnp.float32),
        "spatial_basis": bell_draw(seeds[1], (S, S), S ** -0.5, 0.1875),
        "temporal_basis": bell_draw(seeds[2], (T_SIZE, T_SIZE), T_SIZE ** -0.5, 0.125),
        "spectral_weight": jnp.clip(jnp.exp(math.log(5.0) - 3.218876 * jax.random.uniform(seeds[3], (S, T_SIZE), jnp.float32) ** block_levels(seeds[3], (S, T_SIZE), ((1, 64),), -0.2, 0.2)), 0.2, 5.0),
        "pierce_nodes": with_ends(jax.random.randint(seeds[4], (DIRS, NTB, KNN, STATIONS), 0, S), jax.random.fold_in(seeds[4], 1), 0, S - 1).astype(jnp.int32),
        "pierce_weights": jnp.clip(0.2 + 0.8 * jax.random.uniform(seeds[5], (DIRS, NTB, KNN, STATIONS), jnp.float32) ** block_levels(seeds[5], (DIRS, NTB, KNN, STATIONS), ((0, 4), (1, 8)), -0.2, 0.2), 0.2, 1.0),
    }


def prior_term(field, spatial_basis, temporal_basis, spectral_weight):
    high = lax.Precision.HIGHEST
    start_bf = field.astype(jnp.bfloat16).astype(jnp.float32).reshape(DIRS * S, T_SIZE)
    time_basis = temporal_basis.astype(jnp.float32)
    space_basis = spatial_basis.astype(jnp.float32)
    time_mixed = jnp.dot(start_bf, time_basis, precision=high, preferred_element_type=jnp.float32)
    time_mixed = time_mixed.astype(jnp.bfloat16).astype(jnp.float32).reshape(DIRS, S, T_SIZE)
    space_mixed = jnp.einsum('sk,dsl->dkl', space_basis, time_mixed, precision=high)
    scaled = (spectral_weight[None] * space_mixed).astype(jnp.bfloat16).astype(jnp.float32)
    space_back = jnp.einsum('sk,dkl->dsl', space_basis, scaled, precision=high)
    space_back = space_back.astype(jnp.bfloat16).astype(jnp.float32).reshape(DIRS * S, T_SIZE)
    result = lax.dot_general(space_back, time_basis, (((1,), (1,)), ((), ())), precision=high, preferred_element_type=jnp.float32)
    return result.astype(jnp.bfloat16).astype(jnp.float32).reshape(DIRS, S, T_SIZE)


def pierce_term(field, pierce_nodes, pierce_weights):
    high = lax.Precision.HIGHEST
    node_ids = jnp.arange(S, dtype=jnp.int32)
    blocks = field.reshape(DIRS, S, NTB, TBLK).transpose(0, 2, 1, 3).reshape(DIRS * NTB, S, TBLK)
    nodes_flat = pierce_nodes.reshape(DIRS * NTB, KNN, STATIONS)
    weights_flat = pierce_weights.reshape(DIRS * NTB, KNN, STATIONS)

    def per_block(packed):
        block_field, block_nodes, block_weights = packed
        hits = block_nodes[:, :, None] == node_ids[None, None, :]
        incidence = jnp.sum(jnp.where(hits, block_weights[:, :, None], jnp.zeros_like(block_weights[:, :, None])), axis=0)
        predicted = jnp.dot(incidence, block_field, precision=high)
        return jnp.dot(incidence.T, predicted, precision=high)

    backed = lax.map(per_block, (blocks, nodes_flat, weights_flat))
    return backed.reshape(DIRS, NTB, S, TBLK).transpose(0, 2, 1, 3).reshape(DIRS, S, T_SIZE)


def reference(right_side, spatial_basis, temporal_basis, spectral_weight, pierce_nodes, pierce_weights):
    solution_field = jnp.zeros_like(right_side)
    residual = right_side
    direction = right_side
    res_norm = jnp.sum(residual * residual)
    for iteration in range(ITERS):
        image = prior_term(direction, spatial_basis, temporal_basis, spectral_weight) + pierce_term(direction, pierce_nodes, pierce_weights)
        step_size = res_norm / jnp.sum(direction * image)
        solution_field = solution_field + step_size * direction
        residual = residual - step_size * image
        new_norm = jnp.sum(residual * residual)
        direction = residual + (new_norm / res_norm) * direction
        res_norm = new_norm
    return solution_field, residual
```

```python
import jax
import jax.numpy as jnp
from jax import lax
from jax.experimental import pallas as pl
from jax.experimental.pallas import tpu as pltpu
from jax.sharding import PartitionSpec as P

ITERS = 4
MESH = pl.DeviceIdType.MESH
F32 = jnp.float32
BF16 = jnp.bfloat16
REDUCE_SIZES = (4, 8, 8)


def dot(a, b):
    return jnp.dot(a, b, preferred_element_type=F32)


def swap(a):
    flat = a.reshape(-1, 128)
    return pltpu.roll(flat, 64, 1).reshape(a.shape)


def fold(a):
    return jnp.sum(a.reshape(-1, 8, 128), axis=0)


def total(a):
    return jnp.sum(jnp.sum(a, axis=0, keepdims=True), axis=1, keepdims=True)


def kernel(
    rs_hbm, s_hbm, t_hbm, w_hbm, pn_hbm, pw_hbm,
    xo_ref, ro_ref,
    rs, s4, st, tb, tt4, w_in, pn, pw, pnode, pwgt, g, gt,
    isend, r, x_, d, vb, fsend, frecv, ua, xr, xd, wslot, wf, zb, bsend, brecv, vk,
    pred_r, pred, pb, yacc, red, rr, osend, orecv,
    load_sem, isend_sem, irecv_sem, psend_sem, precv_sem, w1s, w1r, w2s, w2r,
    fs_sem, fr_sem, bs_sem, br_sem, rs_sem, rr_sem, os_sem, or_sem,
):
    z = lax.axis_index("space")
    m = lax.axis_index("tm")
    x = lax.axis_index("dir")
    y, core = m // 2, m % 2
    p = m * 4 + x
    left = lax.broadcasted_iota(jnp.int32, (1, 128), 1) < 64

    def dev(zz, mm, xx):
        return {"space": zz, "tm": mm, "dir": xx}

    def remote(src, dst, ss, rsem, to):
        return pltpu.make_async_remote_copy(
            src_ref=src, dst_ref=dst, send_sem=ss, recv_sem=rsem, device_id=to, device_id_type=MESH
        )

    loads = [
        pltpu.make_async_copy(rs_hbm, rs, load_sem.at[0]),
        pltpu.make_async_copy(pn_hbm, pn, load_sem.at[1]),
        pltpu.make_async_copy(pw_hbm, pw, load_sem.at[2]),
        pltpu.make_async_copy(w_hbm, w_in, load_sem.at[3]),
    ]
    s_loads = [
        pltpu.make_async_copy(s_hbm.at[:, pl.ds(256 * c, 256)], s4.at[c], load_sem.at[4 + c])
        for c in range(4)
    ]
    t_load = pltpu.make_async_copy(t_hbm, tb, load_sem.at[8])
    for copy in loads + s_loads + [t_load]:
        copy.start()

    barrier = pltpu.get_barrier_semaphore()

    def greet(to):
        pl.semaphore_signal(barrier, inc=1, device_id=to, device_id_type=MESH)

    for o in range(1, 32):
        greet(dev(z, (m + o // 4) % 8, (x + o % 4) % 4))
    for o in range(1, 8):
        greet(dev((z + o) % 8, m, x))
    home = z // 2 == x
    for e in range(2):
        for dx in range(4):
            if dx == 0:
                @pl.when(z != 2 * x + e)
                def _():
                    greet(dev(2 * x + e, m, x))
            else:
                greet(dev(2 * x + e, m, (x + dx) % 4))
    for o in range(8):
        if o == 0:
            @pl.when(jnp.logical_not(home))
            def _():
                greet(dev(z, m, z // 2))
        else:
            greet(dev((z + o) % 8, m, z // 2))

    loads[0].wait()
    for e in range(2):
        for h in range(2):
            c = rs[e, :, 128 * h:128 * h + 128]
            top, bottom = c[:64], c[64:]
            isend[4 * e + 2 * h] = jnp.where(left, top, swap(bottom))
            isend[4 * e + 2 * h + 1] = jnp.where(left, swap(top), bottom)
    for copy in loads[1:]:
        copy.wait()

    pl.semaphore_wait(barrier, 54 - 2 * home.astype(jnp.int32))

    for dx in range(4):
        xx = (x + dx) % 4
        for e in range(2):
            slot = 4 * e + xx
            def send():
                remote(isend.at[slot], r.at[z], isend_sem.at[4 * e + dx], irecv_sem,
                       dev(2 * x + e, m, xx)).start()
            if dx == 0:
                pl.when(z != 2 * x + e)(send)

                @pl.when(z == 2 * x + e)
                def _():
                    pltpu.make_async_copy(isend.at[slot], r.at[z], irecv_sem).start()
            else:
                send()
    e_here = z % 2

    @pl.when(home)
    def _():
        for dx in range(1, 4):
            xx = (x + dx) % 4
            remote(pn.at[e_here, xx // 2], pnode, psend_sem.at[dx - 1], precv_sem.at[0], dev(z, m, xx)).start()
            remote(pw.at[e_here, xx // 2], pwgt, psend_sem.at[dx + 2], precv_sem.at[1], dev(z, m, xx)).start()
        pltpu.make_async_copy(pn.at[e_here, x // 2], pnode, precv_sem.at[0]).start()
        pltpu.make_async_copy(pw.at[e_here, x // 2], pwgt, precv_sem.at[1]).start()
    for o in range(1, 8):
        mm = (m + o) % 8
        rows = pl.ds(pl.multiple_of((mm * 4 + x) * 32, 32), 32)
        remote(w_in.at[rows], wslot.at[m], w1s.at[o - 1], w1r, dev(z, mm, x)).start()
    pltpu.make_async_copy(w_in.at[pl.ds(pl.multiple_of(p * 32, 32), 32)], wslot.at[m], w1r).start()

    for c in range(4):
        s_loads[c].wait()
        st[256 * c:256 * c + 256, :] = s4[c].T

    pltpu.make_async_copy(pnode, pnode, precv_sem.at[0]).wait()
    pltpu.make_async_copy(pwgt, pwgt, precv_sem.at[1]).wait()
    nodes, wgts = pnode[...], pwgt[...]
    nodes_t = jnp.concatenate([nodes, nodes], axis=0).astype(F32).T.astype(jnp.int32)
    wgts_t = jnp.concatenate([wgts, wgts], axis=0).T
    for c in range(8):
        ids = lax.broadcasted_iota(jnp.int32, (128, 512), 0) + 128 * c
        acc = jnp.zeros((128, 512), F32)
        for j in range(4):
            acc += jnp.where(nodes[j:j + 1] == ids, wgts[j:j + 1], 0.0)
        gt[128 * c:128 * c + 128, :] = acc.astype(BF16)
        ids = lax.broadcasted_iota(jnp.int32, (512, 128), 1) + 128 * c
        acc = jnp.zeros((512, 128), F32)
        for j in range(4):
            acc += jnp.where(nodes_t[:, j:j + 1] == ids, wgts_t[:, j:j + 1], 0.0)
        g[:, 128 * c:128 * c + 128] = acc.astype(BF16)

    pltpu.make_async_copy(wslot, wslot, w1r).wait()
    own_w = wf.at[z]
    for h in range(2):
        own_w[:, 128 * h:128 * h + 128] = jnp.concatenate([wslot[4 * h + i] for i in range(4)], axis=1)
    for o in range(1, 8):
        remote(wf.at[z], wf.at[z], w2s.at[o - 1], w2r, dev((z + o) % 8, m, x)).start()

    t_load.wait()
    for c in range(4):
        @pl.loop(0, 8)
        def _(i):
            cols = pl.ds(pl.multiple_of(i * 256, 256), 256)
            tt4[c, cols, :] = tb[512 * c:512 * c + 512, cols].T

    x_[...] = jnp.zeros_like(x_)
    d[...] = jnp.zeros_like(d)
    xd[...] = jnp.zeros_like(xd)
    pred[...] = jnp.zeros_like(pred)
    rr[...] = jnp.ones_like(rr)

    pltpu.make_async_copy(r, r, irecv_sem).wait()
    pltpu.make_async_copy(wf.at[pl.ds(0, 7)], wf.at[pl.ds(0, 7)], w2r).wait()

    def reduce_start(kind, step, value):
        n = REDUCE_SIZES[step]
        own = (x, m, z)[step]
        red[kind, step, own] = value
        slot = red.at[kind, step, own]
        for o in range(1, n):
            to = (own + o) % n
            where = (dev(z, m, to), dev(z, to, x), dev(to, m, x))[step]
            remote(slot, slot, rs_sem.at[kind, step], rr_sem.at[kind, step], where).start()

    def reduce_finish(kind, step):
        n = REDUCE_SIZES[step]
        span = red.at[kind, step, pl.ds(0, n - 1)]
        both = remote(span, span, rs_sem.at[kind, step], rr_sem.at[kind, step], dev(z, m, x))
        both.wait_recv()
        both.wait_send()
        return jnp.sum(red[kind, step, 0:n], axis=0)

    def send_row(i, src, dst, ssem, rsem):
        c = (y + i) % 4
        for o in range(8):
            if i == 0 and o == 0:
                continue
            mm = 2 * c + (core + o // 4) % 2
            xx = (x + o % 4) % 4
            remote(src.at[mm * 4 + xx], dst.at[p], ssem, rsem.at[i], dev(z, mm, xx)).start()

    def wait_row(i, buf, rsem):
        span = buf.at[pl.ds(0, 7 if i == 0 else 8)]
        remote(span, span, rsem.at[i], rsem.at[i], dev(z, m, x)).wait_recv()

    def wait_sent(buf, ssem):
        span = buf.at[pl.ds(0, 31)]
        remote(span, span, ssem, ssem, dev(z, m, x)).wait_send()

    @pl.loop(0, ITERS)
    def _(it):
        rv = r[...].reshape(512, 128)
        reduce_start(0, 0, fold(rv * rv))
        rsw = swap(rv)
        vb[:, 0] = jnp.where(left, rv, rsw).astype(BF16).reshape(8, 64, 128)
        vb[:, 1] = jnp.where(left, rsw, rv).astype(BF16).reshape(8, 64, 128)
        vbv = vb[...].reshape(1024, 128)
        for i in range(4):
            c = (y + i) % 4
            u = dot(st[pl.ds(pl.multiple_of(c * 256, 256), 256), :], vbv).reshape(8, 2, 16, 128)
            fsend[pl.ds(c * 8, 8)] = jnp.where(left, u[:, 0], u[:, 1]).astype(BF16)
            send_row(i, fsend, frecv, fs_sem, fr_sem)
        frecv[p] = fsend[p]
        part = reduce_finish(0, 0)
        reduce_start(0, 1, part)
        pred_r[...] = dot(g[...], vbv)
        part = reduce_finish(0, 1)
        reduce_start(0, 2, part)
        for i in range(4):
            c = (y + 4 - i) % 4
            wait_row(i, frecv, fr_sem)
            tiles = frecv[pl.ds(c * 8, 8)].astype(F32)
            swapped = swap(tiles)
            for j in range(4):
                ua[0:16, 128 * j:128 * j + 128] = jnp.where(left, tiles[2 * j], swapped[2 * j + 1]).astype(BF16)
                ua[16:32, 128 * j:128 * j + 128] = jnp.where(left, swapped[2 * j], tiles[2 * j + 1]).astype(BF16)
            xv = dot(ua[...], tb[pl.ds(pl.multiple_of(c * 512, 512), 512), :])
            if i == 0:
                xr[...] = xv
            else:
                xr[...] += xv
        wait_sent(fsend, fs_sem)
        new_norm = total(reduce_finish(0, 2))
        beta = jnp.where(it == 0, 0.0, new_norm / rr[0:1, 0:1])
        rr[...] = jnp.broadcast_to(new_norm, (8, 128))
        pv = pred_r[...] + beta * pred[...]
        pred[...] = pv
        pb[...] = pv.astype(BF16)
        curve = 0.5 * fold(pv * pv)
        for zz in range(8):
            cols = slice(256 * zz, 256 * zz + 256)
            xv = xr[:, cols] + beta * xd[:, cols]
            xd[:, cols] = xv
            wx = wf[zz] * xv
            zb[:, cols] = wx.astype(BF16)
            q = wx * xv
            curve += fold(q[:, :128] + q[:, 128:])
        reduce_start(1, 0, curve)
        zv = zb[...]
        for i in range(4):
            c = (y + i) % 4
            v = dot(zv, tt4[c])
            for j in range(4):
                top, bottom = v[:16, 128 * j:128 * j + 128], v[16:, 128 * j:128 * j + 128]
                bsend[c * 8 + 2 * j] = jnp.where(left, top, swap(bottom)).astype(BF16)
                bsend[c * 8 + 2 * j + 1] = jnp.where(left, swap(top), bottom).astype(BF16)
            send_row(i, bsend, brecv, bs_sem, br_sem)
            if i == 1:
                part = reduce_finish(1, 0)
                reduce_start(1, 1, part)
        brecv[p] = bsend[p]
        part = reduce_finish(1, 1)
        reduce_start(1, 2, part)
        d[...] = r[...] + beta * d[...]
        yacc[...] = dot(gt[...], pb[...])
        for i in range(4):
            c = (y + 4 - i) % 4
            wait_row(i, brecv, br_sem)
            tiles = brecv[pl.ds(c * 8, 8)].astype(F32)
            swapped = swap(tiles)
            vk[:, 0] = jnp.where(left, tiles, swapped).astype(BF16)
            vk[:, 1] = jnp.where(left, swapped, tiles).astype(BF16)
            yacc[...] += dot(s4[c], vk[...].reshape(256, 128))
        wait_sent(bsend, bs_sem)
        alpha = rr[0:1, 0:1] / total(reduce_finish(1, 2))
        ya = yacc[...].reshape(8, 2, 64, 128)
        image = jnp.where(left, ya[:, 0], ya[:, 1])
        x_[...] += alpha * d[...]
        r[...] -= alpha * image

    xv, rv = x_[...], r[...]
    xs, rsw = swap(xv), swap(rv)
    osend[:, 0:64] = jnp.where(left, xv, rsw).astype(BF16)
    osend[:, 64:128] = jnp.where(left, xs, rv).astype(BF16)
    slot_out = (z % 2) * 4 + x
    for o in range(8):
        zz = (z + o) % 8

        def send():
            remote(osend.at[zz], orecv.at[slot_out], os_sem.at[o], or_sem, dev(zz, m, z // 2)).start()
        if o == 0:
            pl.when(jnp.logical_not(home))(send)

            @pl.when(home)
            def _():
                pltpu.make_async_copy(osend.at[zz], orecv.at[slot_out], or_sem).start()
        else:
            send()

    def sent(src, sem):
        remote(src, src, sem, sem, dev(z, m, x)).wait_send()

    for dx in range(4):
        for e in range(2):
            if dx == 0:
                @pl.when(z != 2 * x + e)
                def _():
                    sent(isend.at[0], isend_sem.at[4 * e + dx])
            else:
                sent(isend.at[0], isend_sem.at[4 * e + dx])

    @pl.when(home)
    def _():
        for dx in range(1, 4):
            sent(pn.at[0, 0], psend_sem.at[dx - 1])
            sent(pw.at[0, 0], psend_sem.at[dx + 2])
    for o in range(1, 8):
        sent(w_in.at[pl.ds(0, 32)], w1s.at[o - 1])
        sent(wf.at[0], w2s.at[o - 1])

    pltpu.make_async_copy(orecv, orecv, or_sem).wait()
    for e in range(2):
        for h in range(2):
            a = orecv[4 * e + 2 * h].astype(F32)
            b = orecv[4 * e + 2 * h + 1].astype(F32)
            xo_ref[e, :, 128 * h:128 * h + 128] = jnp.where(left, a, swap(b))
            ro_ref[e, :, 128 * h:128 * h + 128] = jnp.where(left, swap(a), b)
    for o in range(8):
        if o == 0:
            @pl.when(jnp.logical_not(home))
            def _():
                sent(osend.at[0], os_sem.at[o])
        else:
            sent(osend.at[0], os_sem.at[o])


def per_device(right_side, spatial_basis, temporal_basis, spectral_weight, pierce_nodes, pierce_weights):
    vm = pltpu.VMEM
    dma = pltpu.SemaphoreType.DMA
    scratch = [
        vm((2, 128, 256), F32),
        vm((4, 1024, 256), BF16),
        vm((1024, 1024), BF16),
        vm((2048, 2048), BF16),
        vm((4, 2048, 512), BF16),
        vm((1024, 32), F32),
        vm((2, 2, 4, 512), jnp.int32),
        vm((2, 2, 4, 512), F32),
        vm((4, 512), jnp.int32),
        vm((4, 512), F32),
        vm((512, 1024), BF16),
        vm((1024, 512), BF16),
        vm((8, 64, 128), F32),
        vm((8, 64, 128), F32),
        vm((8, 64, 128), F32),
        vm((8, 64, 128), F32),
        vm((8, 2, 64, 128), BF16),
        vm((32, 16, 128), BF16),
        vm((32, 16, 128), BF16),
        vm((32, 512), BF16),
        vm((32, 2048), F32),
        vm((32, 2048), F32),
        vm((8, 32, 32), F32),
        vm((8, 32, 256), F32),
        vm((32, 2048), BF16),
        vm((32, 16, 128), BF16),
        vm((32, 16, 128), BF16),
        vm((8, 2, 16, 128), BF16),
        vm((512, 128), F32),
        vm((512, 128), F32),
        vm((512, 128), BF16),
        vm((1024, 128), F32),
        vm((2, 3, 8, 8, 128), F32),
        vm((8, 128), F32),
        vm((8, 128, 128), BF16),
        vm((8, 128, 128), BF16),
        dma((9,)),
        dma((8,)),
        dma,
        dma((6,)),
        dma((2,)),
        dma((7,)),
        dma,
        dma((7,)),
        dma,
        dma,
        dma((4,)),
        dma,
        dma((4,)),
        dma((2, 3)),
        dma((2, 3)),
        dma((8,)),
        dma,
    ]
    out = jax.ShapeDtypeStruct(right_side.shape, F32)
    return pl.pallas_call(
        kernel,
        out_shape=(out, out),
        in_specs=[pl.BlockSpec(memory_space=pl.ANY)] * 6,
        out_specs=(pl.BlockSpec(memory_space=pltpu.VMEM),) * 2,
        scratch_shapes=scratch,
        name="cg",
        compiler_params=pltpu.CompilerParams(
            collective_id=0, has_side_effects=True, vmem_limit_bytes=56 * 2**20
        ),
    )(right_side, spatial_basis, temporal_basis, spectral_weight, pierce_nodes, pierce_weights)


def solution(mesh):
    placed = (
        P("dir", "space", "tm"),
        P(),
        P(),
        P(None, ("space", "tm")),
        P("dir", "tm", None, None),
        P("dir", "tm", None, None),
    )
    return jax.shard_map(
        per_device,
        mesh=mesh,
        in_specs=placed,
        out_specs=(P("dir", "space", "tm"), P("dir", "space", "tm")),
        check_vma=False,
    )
```

```python
import jax
import jax.numpy as jnp
from jax import lax
from jax.experimental import pallas as pl
from jax.experimental.pallas import tpu as pltpu
from jax.sharding import PartitionSpec as P

ITERS = 4
MESH = pl.DeviceIdType.MESH
F32 = jnp.float32
BF16 = jnp.bfloat16
ROWS = (2, 1, 3, 0)


def dot(a, b):
    return jnp.dot(a, b, preferred_element_type=F32)


def swap(a):
    flat = a.reshape(-1, 128)
    return pltpu.roll(flat, 64, 1).reshape(a.shape)


def fold(a):
    return jnp.sum(a.reshape(-1, 8, 128), axis=0)


def total(a):
    return jnp.sum(jnp.sum(a, axis=0, keepdims=True), axis=1, keepdims=True)


def kernel(
    rs_hbm, s_hbm, t_hbm, w_hbm, pn_hbm, pw_hbm,
    xo_ref, ro_ref,
    rs, s4, st, tb, tt4, w_in, pn, pw, pnode, pwgt, g, gt,
    w_cols, isend, i1, i2, r, x_, d, q, vb, fsend, frecv, ua, xr, xd, wslot, wf, zb, bsend, brecv, vk,
    pred_r, pred, pb, yacc, red, scal, osend, orecv,
    load_sem, i1s, i1r, i2s, i2r, psend_sem, precv_sem, w1s, w1r, w2s, w2r,
    fs_sem, fr_sem, bs_sem, br_sem, rs_sem, rr_sem, os_sem, or_sem,
):
    z = lax.axis_index("space")
    m = lax.axis_index("tm")
    x = lax.axis_index("dir")
    y, core = m // 2, m % 2
    p = m * 4 + x
    left = lax.broadcasted_iota(jnp.int32, (1, 128), 1) < 64

    def dev(zz, mm, xx):
        return {"space": zz, "tm": mm, "dir": xx}

    def remote(src, dst, ss, rsem, to):
        return pltpu.make_async_remote_copy(
            src_ref=src, dst_ref=dst, send_sem=ss, recv_sem=rsem, device_id=to, device_id_type=MESH
        )

    loads = [
        pltpu.make_async_copy(rs_hbm, rs, load_sem.at[0]),
        pltpu.make_async_copy(pn_hbm, pn, load_sem.at[1]),
        pltpu.make_async_copy(pw_hbm, pw, load_sem.at[2]),
        pltpu.make_async_copy(w_hbm, w_in, load_sem.at[3]),
    ]
    s_loads = [
        pltpu.make_async_copy(s_hbm.at[:, pl.ds(256 * c, 256)], s4.at[c], load_sem.at[4 + c])
        for c in range(4)
    ]
    t_load = pltpu.make_async_copy(t_hbm, tb, load_sem.at[8])
    for copy in loads + s_loads + [t_load]:
        copy.start()

    barrier = pltpu.get_barrier_semaphore()

    def greet(to):
        pl.semaphore_signal(barrier, inc=1, device_id=to, device_id_type=MESH)

    for o in range(1, 32):
        greet(dev(z, (m + o // 4) % 8, (x + o % 4) % 4))
    for o in range(2, 16):
        greet(dev((z + o // 2) % 8, 2 * y + (core + o) % 2, x))
    home = z // 2 == x
    for e in range(2):
        for dx in range(4):
            if dx == 0:
                @pl.when(z != 2 * x + e)
                def _():
                    greet(dev(2 * x + e, m, x))
            else:
                greet(dev(2 * x + e, m, (x + dx) % 4))
    for o in range(8):
        if o == 0:
            @pl.when(jnp.logical_not(home))
            def _():
                greet(dev(z, m, z // 2))
        else:
            greet(dev((z + o) % 8, m, z // 2))

    loads[0].wait()
    for h in range(2):
        for e in range(2):
            c = rs[e, :, 128 * h:128 * h + 128]
            top, bottom = c[:64], c[64:]
            isend[2 * h, e] = jnp.where(left, top, swap(bottom)).astype(BF16)
            isend[2 * h + 1, e] = jnp.where(left, swap(top), bottom).astype(BF16)
    i1[pl.ds(2 * x, 2)] = isend[x]
    for copy in loads[1:]:
        copy.wait()

    pl.semaphore_wait(barrier, 61 - 2 * home.astype(jnp.int32))

    for dx in (2, 1, 3):
        xx = (x + dx) % 4
        remote(isend.at[xx], i1.at[pl.ds(2 * x, 2)], i1s.at[dx - 1], i1r.at[dx - 1], dev(z, m, xx)).start()
    e_here = z % 2

    @pl.when(home)
    def _():
        for dx in range(1, 4):
            xx = (x + dx) % 4
            remote(pn.at[e_here, xx // 2], pnode, psend_sem.at[dx - 1], precv_sem.at[0], dev(z, m, xx)).start()
            remote(pw.at[e_here, xx // 2], pwgt, psend_sem.at[dx + 2], precv_sem.at[1], dev(z, m, xx)).start()
        pltpu.make_async_copy(pn.at[e_here, x // 2], pnode, precv_sem.at[0]).start()
        pltpu.make_async_copy(pw.at[e_here, x // 2], pwgt, precv_sem.at[1]).start()
    w_cols[...] = w_in[...].T.reshape(32, 32, 32)
    for o in range(1, 8):
        mm = (m + o) % 8
        remote(w_cols.at[mm * 4 + x], wslot.at[m], w1s.at[o - 1], w1r, dev(z, mm, x)).start()
    pltpu.make_async_copy(w_cols.at[p], wslot.at[m], w1r).start()

    def forward(xx):
        for e in range(2):
            zz = 2 * xx + e

            @pl.when(zz != z)
            def _():
                remote(i1.at[zz], i2.at[z], i2s.at[(zz + 7 - z) % 8], i2r, dev(zz, m, x)).start()

            @pl.when(zz == z)
            def _():
                pltpu.make_async_copy(i1.at[zz], i2.at[z], i2r).start()

    forward(x)
    for c in range(4):
        s_loads[c].wait()
        st[256 * c:256 * c + 256, :] = s4[c].T
    for dx in (1, 3, 2):
        xx = (x + 4 - dx) % 4
        span = i1.at[pl.ds(2 * xx, 2)]
        remote(span, span, i1s.at[dx - 1], i1r.at[dx - 1], dev(z, m, x)).wait_recv()
        forward(xx)

    pltpu.make_async_copy(pnode, pnode, precv_sem.at[0]).wait()
    pltpu.make_async_copy(pwgt, pwgt, precv_sem.at[1]).wait()
    nodes, wgts = pnode[...], pwgt[...]
    nodes_t = jnp.concatenate([nodes, nodes], axis=0).astype(F32).T.astype(jnp.int32)
    wgts_t = jnp.concatenate([wgts, wgts], axis=0).T
    for c in range(8):
        ids = lax.broadcasted_iota(jnp.int32, (128, 512), 0) + 128 * c
        acc = jnp.zeros((128, 512), F32)
        for j in range(4):
            acc += jnp.where(nodes[j:j + 1] == ids, wgts[j:j + 1], 0.0)
        gt[128 * c:128 * c + 128, :] = acc.astype(BF16)
        ids = lax.broadcasted_iota(jnp.int32, (512, 128), 1) + 128 * c
        acc = jnp.zeros((512, 128), F32)
        for j in range(4):
            acc += jnp.where(nodes_t[:, j:j + 1] == ids, wgts_t[:, j:j + 1], 0.0)
        g[:, 128 * c:128 * c + 128] = acc.astype(BF16)

    pltpu.make_async_copy(wslot, wslot, w1r).wait()
    own_w = wf.at[z]
    for h in range(2):
        own_w[:, 128 * h:128 * h + 128] = jnp.concatenate([wslot[4 * h + i] for i in range(4)], axis=1)
    for o in range(1, 8):
        remote(wf.at[z], wf.at[z], w2s.at[o - 1], w2r, dev((z + o) % 8, m, x)).start()

    t_load.wait()
    for c in range(4):
        @pl.loop(0, 8)
        def _(i):
            cols = pl.ds(pl.multiple_of(i * 256, 256), 256)
            tt4[c, cols, :] = tb[512 * c:512 * c + 512, cols].T

    for ref in (x_, d, q, xr, xd, pred_r, pred):
        ref[...] = jnp.zeros_like(ref)
    scal[...] = jnp.ones_like(scal)

    pltpu.make_async_copy(i2, i2, i2r).wait()
    r[...] = i2[...].astype(F32)

    def reduce_start(par, step, value):
        own = (y * 4 + x, z * 2 + core)[step]
        slot = red.at[par, step, own]
        slot[...] = value
        for o in range(1, 16):
            if step == 0:
                where = dev(z, 2 * ((y + o // 4) % 4) + core, (x + o % 4) % 4)
            else:
                where = dev((z + o // 2) % 8, 2 * y + (core + o) % 2, x)
            remote(slot, slot, rs_sem.at[par, step], rr_sem.at[par, step], where).start()

    def reduce_finish(par, step):
        span = red.at[par, step, pl.ds(0, 15)]
        both = remote(span, span, rs_sem.at[par, step], rr_sem.at[par, step], dev(z, m, x))
        both.wait_recv()
        both.wait_send()
        return jnp.sum(red[par, step], axis=0)

    def send_row(dy, src, dst, ssem, rsem):
        c = (y + dy) % 4
        for o in range(8):
            if dy == 0 and o == 0:
                continue
            mm = 2 * c + (core + o // 4) % 2
            xx = (x + o % 4) % 4
            remote(src.at[mm * 4 + xx], dst.at[p], ssem, rsem.at[dy], dev(z, mm, xx)).start()

    def wait_row(dy, buf, rsem):
        span = buf.at[pl.ds(0, 7 if dy == 0 else 8)]
        remote(span, span, rsem.at[dy], rsem.at[dy], dev(z, m, x)).wait_recv()

    def wait_sent(buf, ssem):
        span = buf.at[pl.ds(0, 31)]
        remote(span, span, ssem, ssem, dev(z, m, x)).wait_send()

    @pl.loop(0, ITERS)
    def _(it):
        par = it % 2
        rv = r[...].reshape(512, 128)
        rsw = swap(rv)
        vb[:, 0] = jnp.where(left, rv, rsw).astype(BF16).reshape(8, 64, 128)
        vb[:, 1] = jnp.where(left, rsw, rv).astype(BF16).reshape(8, 64, 128)
        vbv = vb[...].reshape(1024, 128)
        for dy in ROWS:
            c = (y + dy) % 4
            u = dot(st[pl.ds(pl.multiple_of(c * 256, 256), 256), :], vbv).reshape(8, 2, 16, 128)
            fsend[pl.ds(c * 8, 8)] = jnp.where(left, u[:, 0], u[:, 1]).astype(BF16)
            send_row(dy, fsend, frecv, fs_sem, fr_sem)
        frecv[p] = fsend[p]
        beta = scal[2, 0:1, 0:1]
        xd[...] = xr[...] + beta * xd[...]
        pold = pred_r[...] + beta * pred[...]
        pred[...] = pold
        pnew = dot(g[...], vbv)
        pred_r[...] = pnew
        pb[...] = pnew.astype(BF16)
        norm = fold(rv * rv)
        suma = 0.5 * fold(pnew * pnew)
        sumb = 0.5 * fold(pnew * pold)
        for n, dy in enumerate(ROWS):
            c = (y + 4 - dy) % 4
            wait_row(dy, frecv, fr_sem)
            tiles = frecv[pl.ds(c * 8, 8)].astype(F32)
            swapped = swap(tiles)
            for j in range(4):
                ua[0:16, 128 * j:128 * j + 128] = jnp.where(left, tiles[2 * j], swapped[2 * j + 1]).astype(BF16)
                ua[16:32, 128 * j:128 * j + 128] = jnp.where(left, swapped[2 * j], tiles[2 * j + 1]).astype(BF16)
            xv = dot(ua[...], tb[pl.ds(pl.multiple_of(c * 512, 512), 512), :])
            if n == 0:
                xr[...] = xv
            else:
                xr[...] += xv
        wait_sent(fsend, fs_sem)

        @pl.when(it == 0)
        def _():
            pltpu.make_async_copy(wf.at[pl.ds(0, 7)], wf.at[pl.ds(0, 7)], w2r).wait()

        for zz in range(8):
            cols = slice(256 * zz, 256 * zz + 256)
            xv = xr[:, cols]
            wx = wf[zz] * xv
            zb[:, cols] = wx.astype(BF16)
            qa, qb = wx * xv, wx * xd[:, cols]
            suma += fold(qa[:, :128] + qa[:, 128:])
            sumb += fold(qb[:, :128] + qb[:, 128:])
        row = lax.broadcasted_iota(jnp.int32, (8, 128), 0)
        one = [jnp.sum(part, axis=0, keepdims=True) for part in (norm, suma, sumb)]
        reduce_start(par, 0, jnp.where(row == 0, one[0], jnp.where(row == 1, one[1], one[2])))
        zv = zb[...]
        for n, dy in enumerate(ROWS):
            c = (y + dy) % 4
            v = dot(zv, tt4[c])
            for j in range(4):
                top, bottom = v[:16, 128 * j:128 * j + 128], v[16:, 128 * j:128 * j + 128]
                bsend[c * 8 + 2 * j] = jnp.where(left, top, swap(bottom)).astype(BF16)
                bsend[c * 8 + 2 * j + 1] = jnp.where(left, swap(top), bottom).astype(BF16)
            send_row(dy, bsend, brecv, bs_sem, br_sem)
            if n == 2:
                part = reduce_finish(par, 0)
                reduce_start(par, 1, part)
        brecv[p] = bsend[p]
        yacc[...] = dot(gt[...], pb[...])
        for dy in ROWS:
            c = (y + 4 - dy) % 4
            wait_row(dy, brecv, br_sem)
            tiles = brecv[pl.ds(c * 8, 8)].astype(F32)
            swapped = swap(tiles)
            vk[:, 0] = jnp.where(left, tiles, swapped).astype(BF16)
            vk[:, 1] = jnp.where(left, swapped, tiles).astype(BF16)
            yacc[...] += dot(s4[c], vk[...].reshape(256, 128))
        wait_sent(bsend, bs_sem)
        sums = jnp.sum(reduce_finish(par, 1), axis=1, keepdims=True)
        rr, ra, rb = sums[0:1], sums[1:2], sums[2:3]
        beta = jnp.where(it == 0, 0.0, rr / scal[0, 0:1, 0:1])
        curve = ra + beta * (2.0 * rb + beta * scal[1, 0:1, 0:1])
        alpha = rr / curve
        scal[0] = jnp.broadcast_to(rr, (8, 128))
        scal[1] = jnp.broadcast_to(curve, (8, 128))
        scal[2] = jnp.broadcast_to(beta, (8, 128))
        ya = yacc[...].reshape(8, 2, 64, 128)
        qv = jnp.where(left, ya[:, 0], ya[:, 1]) + beta * q[...]
        q[...] = qv
        dv = r[...] + beta * d[...]
        d[...] = dv
        x_[...] += alpha * dv
        r[...] -= alpha * qv

    xv, rv = x_[...], r[...]
    xs, rsw = swap(xv), swap(rv)
    osend[:, 0:64] = jnp.where(left, xv, rsw).astype(BF16)
    osend[:, 64:128] = jnp.where(left, xs, rv).astype(BF16)
    slot_out = (z % 2) * 4 + x
    for o in range(8):
        zz = (z + o) % 8

        def send():
            remote(osend.at[zz], orecv.at[slot_out], os_sem.at[o], or_sem, dev(zz, m, z // 2)).start()
        if o == 0:
            pl.when(jnp.logical_not(home))(send)

            @pl.when(home)
            def _():
                pltpu.make_async_copy(osend.at[zz], orecv.at[slot_out], or_sem).start()
        else:
            send()

    def sent(src, sem):
        remote(src, src, sem, sem, dev(z, m, x)).wait_send()

    for o in range(3):
        sent(isend.at[0], i1s.at[o])
    for o in range(7):
        sent(i1.at[0], i2s.at[o])

    @pl.when(home)
    def _():
        for dx in range(1, 4):
            sent(pn.at[0, 0], psend_sem.at[dx - 1])
            sent(pw.at[0, 0], psend_sem.at[dx + 2])
    for o in range(1, 8):
        sent(w_cols.at[0], w1s.at[o - 1])
        sent(wf.at[0], w2s.at[o - 1])

    pltpu.make_async_copy(orecv, orecv, or_sem).wait()
    for e in range(2):
        for h in range(2):
            a = orecv[4 * e + 2 * h].astype(F32)
            b = orecv[4 * e + 2 * h + 1].astype(F32)
            xo_ref[e, :, 128 * h:128 * h + 128] = jnp.where(left, a, swap(b))
            ro_ref[e, :, 128 * h:128 * h + 128] = jnp.where(left, swap(a), b)
    for o in range(8):
        if o == 0:
            @pl.when(jnp.logical_not(home))
            def _():
                sent(osend.at[0], os_sem.at[o])
        else:
            sent(osend.at[0], os_sem.at[o])


def per_device(right_side, spatial_basis, temporal_basis, spectral_weight, pierce_nodes, pierce_weights):
    vm = pltpu.VMEM
    dma = pltpu.SemaphoreType.DMA
    scratch = [
        vm((2, 128, 256), F32),
        vm((4, 1024, 256), BF16),
        vm((1024, 1024), BF16),
        vm((2048, 2048), BF16),
        vm((4, 2048, 512), BF16),
        vm((32, 1024), F32),
        vm((2, 2, 4, 512), jnp.int32),
        vm((2, 2, 4, 512), F32),
        vm((4, 512), jnp.int32),
        vm((4, 512), F32),
        vm((512, 1024), BF16),
        vm((1024, 512), BF16),
        vm((32, 32, 32), F32),
        vm((4, 2, 64, 128), BF16),
        vm((8, 64, 128), BF16),
        vm((8, 64, 128), BF16),
        vm((8, 64, 128), F32),
        vm((8, 64, 128), F32),
        vm((8, 64, 128), F32),
        vm((8, 64, 128), F32),
        vm((8, 2, 64, 128), BF16),
        vm((32, 16, 128), BF16),
        vm((32, 16, 128), BF16),
        vm((32, 512), BF16),
        vm((32, 2048), F32),
        vm((32, 2048), F32),
        vm((8, 32, 32), F32),
        vm((8, 32, 256), F32),
        vm((32, 2048), BF16),
        vm((32, 16, 128), BF16),
        vm((32, 16, 128), BF16),
        vm((8, 2, 16, 128), BF16),
        vm((512, 128), F32),
        vm((512, 128), F32),
        vm((512, 128), BF16),
        vm((1024, 128), F32),
        vm((2, 2, 16, 8, 128), F32),
        vm((3, 8, 128), F32),
        vm((8, 128, 128), BF16),
        vm((8, 128, 128), BF16),
        dma((9,)),
        dma((3,)),
        dma((3,)),
        dma((7,)),
        dma,
        dma((6,)),
        dma((2,)),
        dma((7,)),
        dma,
        dma((7,)),
        dma,
        dma,
        dma((4,)),
        dma,
        dma((4,)),
        dma((2, 2)),
        dma((2, 2)),
        dma((8,)),
        dma,
    ]
    out = jax.ShapeDtypeStruct(right_side.shape, F32)
    return pl.pallas_call(
        kernel,
        out_shape=(out, out),
        in_specs=[pl.BlockSpec(memory_space=pl.ANY)] * 6,
        out_specs=(pl.BlockSpec(memory_space=pltpu.VMEM),) * 2,
        scratch_shapes=scratch,
        name="cg",
        compiler_params=pltpu.CompilerParams(
            collective_id=0, has_side_effects=True, vmem_limit_bytes=56 * 2**20
        ),
    )(right_side, spatial_basis, temporal_basis, spectral_weight.T, pierce_nodes, pierce_weights)


def solution(mesh):
    placed = (
        P("dir", "space", "tm"),
        P(),
        P(),
        P(None, ("space", "tm")),
        P("dir", "tm", None, None),
        P("dir", "tm", None, None),
    )
    return jax.shard_map(
        per_device,
        mesh=mesh,
        in_specs=placed,
        out_specs=(P("dir", "space", "tm"), P("dir", "space", "tm")),
        check_vma=False,
    )
```

```python
import jax
import jax.numpy as jnp
from jax import lax
from jax.experimental import pallas as pl
from jax.experimental.pallas import tpu as pltpu
from jax.sharding import PartitionSpec as P

ITERS = 4
MESH = pl.DeviceIdType.MESH
F32 = jnp.float32
BF16 = jnp.bfloat16
ROWS = (2, 1, 3, 0)


def dot(a, b):
    return jnp.dot(a, b, preferred_element_type=F32)


def swap(a):
    flat = a.reshape(-1, 128)
    return pltpu.roll(flat, 64, 1).reshape(a.shape)


def fold(a):
    return jnp.sum(a.reshape(-1, 8, 128), axis=0)


def total(a):
    return jnp.sum(jnp.sum(a, axis=0, keepdims=True), axis=1, keepdims=True)


def kernel(
    rs_hbm, s_hbm, t_hbm, w_hbm, pn_hbm, pw_hbm,
    xo_ref, ro_ref,
    rs, s4, st, tb, tt4, w_in, pn, pw, pnode, pwgt, g, gt,
    w_cols, isend, i1, i2, im, r, q, vb, fsend, frecv, ua, xv_, xm, xq, xd, wslot, wf, zb, bsend, brecv, vk,
    pr, pq, pd, pb, yacc, red, scal, xb, db, qb, osend, orecv, olast,
    load_sem, i1s, i1r, i2s, i2r, psend_sem, precv_sem, w1s, w1r, w2s, w2r,
    fs_sem, fr_sem, bs_sem, br_sem, rs_sem, rr_sem, os_sem, or_sem,
):
    z = lax.axis_index("space")
    m = lax.axis_index("tm")
    x = lax.axis_index("dir")
    y, core = m // 2, m % 2
    p = m * 4 + x
    left = lax.broadcasted_iota(jnp.int32, (1, 128), 1) < 64

    def dev(zz, mm, xx):
        return {"space": zz, "tm": mm, "dir": xx}

    def remote(src, dst, ss, rsem, to):
        return pltpu.make_async_remote_copy(
            src_ref=src, dst_ref=dst, send_sem=ss, recv_sem=rsem, device_id=to, device_id_type=MESH
        )

    loads = [
        pltpu.make_async_copy(rs_hbm, rs, load_sem.at[0]),
        pltpu.make_async_copy(pn_hbm, pn, load_sem.at[1]),
        pltpu.make_async_copy(pw_hbm, pw, load_sem.at[2]),
        pltpu.make_async_copy(w_hbm, w_in, load_sem.at[3]),
    ]
    s_loads = [
        pltpu.make_async_copy(s_hbm.at[:, pl.ds(256 * c, 256)], s4.at[c], load_sem.at[4 + c])
        for c in range(4)
    ]
    t_load = pltpu.make_async_copy(t_hbm, tb, load_sem.at[8])
    for copy in loads + s_loads + [t_load]:
        copy.start()

    barrier = pltpu.get_barrier_semaphore()

    def greet(to):
        pl.semaphore_signal(barrier, inc=1, device_id=to, device_id_type=MESH)

    for o in range(1, 32):
        greet(dev(z, (m + o // 4) % 8, (x + o % 4) % 4))
    for o in range(2, 16):
        greet(dev((z + o // 2) % 8, 2 * y + (core + o) % 2, x))
    home = z // 2 == x
    for e in range(2):
        for dx in range(4):
            if dx == 0:
                @pl.when(z != 2 * x + e)
                def _():
                    greet(dev(2 * x + e, m, x))
            else:
                greet(dev(2 * x + e, m, (x + dx) % 4))
    for o in range(8):
        if o == 0:
            @pl.when(jnp.logical_not(home))
            def _():
                greet(dev(z, m, z // 2))
        else:
            greet(dev((z + o) % 8, m, z // 2))

    loads[0].wait()
    for h in range(2):
        for e in range(2):
            c = rs[e, :, 128 * h:128 * h + 128]
            top, bottom = c[:64], c[64:]
            isend[2 * h, e] = jnp.where(left, top, swap(bottom)).astype(BF16)
            isend[2 * h + 1, e] = jnp.where(left, swap(top), bottom).astype(BF16)
    i1[pl.ds(2 * x, 2)] = isend[x]
    for copy in loads[1:]:
        copy.wait()
    w_cols[...] = w_in[...].T.reshape(32, 32, 32)

    pl.semaphore_wait(barrier, 61 - 2 * home.astype(jnp.int32))

    for dx in (2, 1, 3):
        xx = (x + dx) % 4
        remote(isend.at[xx], i1.at[pl.ds(2 * x, 2)], i1s.at[dx - 1], i1r.at[dx - 1], dev(z, m, xx)).start()
    e_here = z % 2

    @pl.when(home)
    def _():
        for dx in range(1, 4):
            xx = (x + dx) % 4
            remote(pn.at[e_here, xx // 2], pnode, psend_sem.at[dx - 1], precv_sem.at[0], dev(z, m, xx)).start()
            remote(pw.at[e_here, xx // 2], pwgt, psend_sem.at[dx + 2], precv_sem.at[1], dev(z, m, xx)).start()
        pltpu.make_async_copy(pn.at[e_here, x // 2], pnode, precv_sem.at[0]).start()
        pltpu.make_async_copy(pw.at[e_here, x // 2], pwgt, precv_sem.at[1]).start()
    for o in range(1, 8):
        mm = (m + o) % 8
        remote(w_cols.at[mm * 4 + x], wslot.at[m], w1s.at[o - 1], w1r, dev(z, mm, x)).start()
    pltpu.make_async_copy(w_cols.at[p], wslot.at[m], w1r).start()

    def forward(xx):
        for e in range(2):
            zz = 2 * xx + e

            @pl.when(zz != z)
            def _():
                remote(i1.at[zz], i2.at[z], i2s.at[(zz + 7 - z) % 8], i2r, dev(zz, m, x)).start()

            @pl.when(zz == z)
            def _():
                pltpu.make_async_copy(i1.at[zz], i2.at[z], i2r).start()

    forward(x)
    for c in range(4):
        s_loads[c].wait()
        st[256 * c:256 * c + 256, :] = s4[c].T
    for dx in (1, 3, 2):
        xx = (x + 4 - dx) % 4
        span = i1.at[pl.ds(2 * xx, 2)]
        remote(span, span, i1s.at[dx - 1], i1r.at[dx - 1], dev(z, m, x)).wait_recv()
        forward(xx)

    pltpu.make_async_copy(wslot, wslot, w1r).wait()
    own_w = wf.at[z]
    for h in range(2):
        own_w[:, 128 * h:128 * h + 128] = jnp.concatenate([wslot[4 * h + i] for i in range(4)], axis=1)
    for o in range(1, 8):
        remote(wf.at[z], wf.at[z], w2s.at[o - 1], w2r, dev((z + o) % 8, m, x)).start()

    for ref in (r, q, xm, xq, xd, pr, pq, pd, xb, db, qb):
        ref[...] = jnp.zeros_like(ref)
    scal[0:2] = jnp.ones((2, 8, 128), F32)
    scal[2] = jnp.full((8, 128), -1.0, F32)
    scal[3] = jnp.zeros((8, 128), F32)

    pltpu.make_async_copy(pnode, pnode, precv_sem.at[0]).wait()
    pltpu.make_async_copy(pwgt, pwgt, precv_sem.at[1]).wait()
    nodes, wgts = pnode[...], pwgt[...]
    nodes_t = jnp.concatenate([nodes, nodes], axis=0).astype(F32).T.astype(jnp.int32)
    wgts_t = jnp.concatenate([wgts, wgts], axis=0).T
    for c in range(8):
        ids = lax.broadcasted_iota(jnp.int32, (128, 512), 0) + 128 * c
        acc = jnp.zeros((128, 512), F32)
        for j in range(4):
            acc += jnp.where(nodes[j:j + 1] == ids, wgts[j:j + 1], 0.0)
        gt[128 * c:128 * c + 128, :] = acc.astype(BF16)
        ids = lax.broadcasted_iota(jnp.int32, (512, 128), 1) + 128 * c
        acc = jnp.zeros((512, 128), F32)
        for j in range(4):
            acc += jnp.where(nodes_t[:, j:j + 1] == ids, wgts_t[:, j:j + 1], 0.0)
        g[:, 128 * c:128 * c + 128] = acc.astype(BF16)

    def transpose(c):
        @pl.loop(0, 8)
        def _(i):
            cols = pl.ds(pl.multiple_of(i * 256, 256), 256)
            tt4[c, cols, :] = tb[512 * c:512 * c + 512, cols].T

    t_load.wait()
    for c in range(2):
        transpose(c)

    pltpu.make_async_copy(i2, i2, i2r).wait()
    im[...] = i2[...].astype(F32)

    def reduce_start(par, step, value):
        own = (y * 4 + x, z * 2 + core)[step]
        slot = red.at[par, step, own]
        slot[...] = value
        for o in range(1, 16):
            if step == 0:
                where = dev(z, 2 * ((y + o // 4) % 4) + core, (x + o % 4) % 4)
            else:
                where = dev((z + o // 2) % 8, 2 * y + (core + o) % 2, x)
            remote(slot, slot, rs_sem.at[par, step], rr_sem.at[par, step], where).start()

    def reduce_finish(par, step):
        span = red.at[par, step, pl.ds(0, 15)]
        both = remote(span, span, rs_sem.at[par, step], rr_sem.at[par, step], dev(z, m, x))
        both.wait_recv()
        both.wait_send()
        return jnp.sum(red[par, step], axis=0)

    def send_row(dy, src, dst, ssem, rsem):
        c = (y + dy) % 4
        for o in range(8):
            if dy == 0 and o == 0:
                continue
            mm = 2 * c + (core + o // 4) % 2
            xx = (x + o % 4) % 4
            remote(src.at[mm * 4 + xx], dst.at[p], ssem, rsem.at[dy], dev(z, mm, xx)).start()

    def wait_row(dy, buf, rsem):
        span = buf.at[pl.ds(0, 7 if dy == 0 else 8)]
        remote(span, span, rsem.at[dy], rsem.at[dy], dev(z, m, x)).wait_recv()

    def wait_sent(buf, ssem):
        span = buf.at[pl.ds(0, 31)]
        remote(span, span, ssem, ssem, dev(z, m, x)).wait_send()

    def scalars(j):
        sums = jnp.sum(reduce_finish(j % 2, 1), axis=1, keepdims=True)
        rr, ra, rb = sums[0:1], sums[1:2], sums[2:3]
        beta = jnp.where(j == 0, 0.0, rr / scal[0, 0:1, 0:1])
        curve = ra + beta * (2.0 * rb + beta * scal[1, 0:1, 0:1])
        for n, value in enumerate((rr, curve, rr / curve, beta)):
            scal[n] = jnp.broadcast_to(value, (8, 128))

    def factors():
        return scal[2, 0:1, 0:1], scal[3, 0:1, 0:1]

    slot_out = (z % 2) * 4 + x

    def ship(src, dst, sem):
        for o in range(8):
            zz = (z + o) % 8

            def send():
                remote(src.at[zz], dst.at[slot_out], os_sem.at[o], sem, dev(zz, m, z // 2)).start()
            if o == 0:
                pl.when(jnp.logical_not(home))(send)

                @pl.when(home)
                def _():
                    pltpu.make_async_copy(src.at[zz], dst.at[slot_out], sem).start()
            else:
                send()

    def shipped(src, dst, sem):
        pltpu.make_async_copy(dst, dst, sem).wait()
        for o in range(8):
            if o == 0:
                @pl.when(jnp.logical_not(home))
                def _():
                    sent(src.at[0], os_sem.at[o])
            else:
                sent(src.at[0], os_sem.at[o])

    def sent(src, sem):
        remote(src, src, sem, sem, dev(z, m, x)).wait_send()

    def advance(tiles, x_out, r_out):
        alpha, beta = factors()
        for e in range(2):
            for h in range(2):
                a, b = tiles[4 * e + 2 * h].astype(F32), tiles[4 * e + 2 * h + 1].astype(F32)
                for part, rows in ((jnp.where(left, a, swap(b)), slice(0, 64)), (jnp.where(left, swap(a), b), slice(64, 128))):
                    at = (e, rows, slice(128 * h, 128 * h + 128))
                    qn = part + beta * qb[at]
                    dn = rs[at] + beta * db[at]
                    qb[at] = qn
                    db[at] = dn
                    x_out[at] = xb[at] + alpha * dn
                    r_out[at] = rs[at] - alpha * qn

    @pl.loop(0, ITERS)
    def _(it):
        par = it % 2
        v = im[...].reshape(512, 128)
        vsw = swap(v)
        vb[:, 0] = jnp.where(left, v, vsw).astype(BF16).reshape(8, 64, 128)
        vb[:, 1] = jnp.where(left, vsw, v).astype(BF16).reshape(8, 64, 128)
        vbv = vb[...].reshape(1024, 128)
        for dy in ROWS:
            c = (y + dy) % 4
            u = dot(st[pl.ds(pl.multiple_of(c * 256, 256), 256), :], vbv).reshape(8, 2, 16, 128)
            fsend[pl.ds(c * 8, 8)] = jnp.where(left, u[:, 0], u[:, 1]).astype(BF16)
            send_row(dy, fsend, frecv, fs_sem, fr_sem)
        frecv[p] = fsend[p]

        @pl.when(it == 0)
        def _():
            for c in range(2, 4):
                transpose(c)

        @pl.when(it > 0)
        def _():
            ship(im, orecv.at[it - 1], or_sem.at[it - 1])

        pv = dot(g[...], vbv)

        @pl.when(it > 0)
        def _():
            scalars(it - 1)

        alpha, beta = factors()
        pold = pr[...] + beta * pd[...]
        pd[...] = pold
        pqn = pv + beta * pq[...]
        pq[...] = pqn
        pnew = pr[...] - alpha * pqn
        pr[...] = pnew
        pb[...] = pnew.astype(BF16)
        qn = v + beta * q[...].reshape(512, 128)
        q[...] = qn.reshape(8, 64, 128)
        rn = r[...].reshape(512, 128) - alpha * qn
        r[...] = rn.reshape(8, 64, 128)
        norm = fold(rn * rn)
        suma = 0.5 * fold(pnew * pnew)
        sumb = 0.5 * fold(pnew * pold)
        xd[...] = xm[...] + beta * xd[...]
        for n, dy in enumerate(ROWS):
            c = (y + 4 - dy) % 4
            wait_row(dy, frecv, fr_sem)
            tiles = frecv[pl.ds(c * 8, 8)].astype(F32)
            swapped = swap(tiles)
            for j in range(4):
                ua[0:16, 128 * j:128 * j + 128] = jnp.where(left, tiles[2 * j], swapped[2 * j + 1]).astype(BF16)
                ua[16:32, 128 * j:128 * j + 128] = jnp.where(left, swapped[2 * j], tiles[2 * j + 1]).astype(BF16)
            xv = dot(ua[...], tb[pl.ds(pl.multiple_of(c * 512, 512), 512), :])
            if n == 0:
                xv_[...] = xv
            else:
                xv_[...] += xv
        wait_sent(fsend, fs_sem)

        @pl.when(it == 0)
        def _():
            pltpu.make_async_copy(wf.at[pl.ds(0, 7)], wf.at[pl.ds(0, 7)], w2r).wait()

        for zz in range(8):
            cols = slice(256 * zz, 256 * zz + 256)
            xqn = xv_[:, cols] + beta * xq[:, cols]
            xq[:, cols] = xqn
            xn = xm[:, cols] - alpha * xqn
            xm[:, cols] = xn
            wx = wf[zz] * xn
            zb[:, cols] = wx.astype(BF16)
            qa, qc = wx * xn, wx * xd[:, cols]
            suma += fold(qa[:, :128] + qa[:, 128:])
            sumb += fold(qc[:, :128] + qc[:, 128:])
        row = lax.broadcasted_iota(jnp.int32, (8, 128), 0)
        one = [jnp.sum(part, axis=0, keepdims=True) for part in (norm, suma, sumb)]
        reduce_start(par, 0, jnp.where(row == 0, one[0], jnp.where(row == 1, one[1], one[2])))
        zv = zb[...]
        for dy in ROWS:
            c = (y + dy) % 4
            w = dot(zv, tt4[c])
            for j in range(4):
                top, bottom = w[:16, 128 * j:128 * j + 128], w[16:, 128 * j:128 * j + 128]
                bsend[c * 8 + 2 * j] = jnp.where(left, top, swap(bottom)).astype(BF16)
                bsend[c * 8 + 2 * j + 1] = jnp.where(left, swap(top), bottom).astype(BF16)
            send_row(dy, bsend, brecv, bs_sem, br_sem)
        brecv[p] = bsend[p]
        yacc[...] = dot(gt[...], pb[...])
        part = reduce_finish(par, 0)
        reduce_start(par, 1, part)

        @pl.when(it > 0)
        def _():
            shipped(im, orecv.at[it - 1], or_sem.at[it - 1])
            advance(orecv.at[it - 1], xb, rs)

        for dy in ROWS:
            c = (y + 4 - dy) % 4
            wait_row(dy, brecv, br_sem)
            tiles = brecv[pl.ds(c * 8, 8)].astype(F32)
            swapped = swap(tiles)
            vk[:, 0] = jnp.where(left, tiles, swapped).astype(BF16)
            vk[:, 1] = jnp.where(left, swapped, tiles).astype(BF16)
            yacc[...] += dot(s4[c], vk[...].reshape(256, 128))
        wait_sent(bsend, bs_sem)
        ya = yacc[...].reshape(8, 2, 64, 128)
        im[...] = jnp.where(left, ya[:, 0], ya[:, 1])

    osend[...] = im[...].astype(BF16)
    ship(osend, olast, or_sem.at[ITERS - 1])
    scalars(ITERS - 1)

    for o in range(3):
        sent(isend.at[0], i1s.at[o])
    for o in range(7):
        sent(i1.at[0], i2s.at[o])

    @pl.when(home)
    def _():
        for dx in range(1, 4):
            sent(pn.at[0, 0], psend_sem.at[dx - 1])
            sent(pw.at[0, 0], psend_sem.at[dx + 2])
    for o in range(1, 8):
        sent(w_cols.at[0], w1s.at[o - 1])
        sent(wf.at[0], w2s.at[o - 1])

    shipped(osend, olast, or_sem.at[ITERS - 1])
    advance(olast, xo_ref, ro_ref)


def per_device(right_side, spatial_basis, temporal_basis, spectral_weight, pierce_nodes, pierce_weights):
    vm = pltpu.VMEM
    dma = pltpu.SemaphoreType.DMA
    scratch = [
        vm((2, 128, 256), F32),
        vm((4, 1024, 256), BF16),
        vm((1024, 1024), BF16),
        vm((2048, 2048), BF16),
        vm((4, 2048, 512), BF16),
        vm((32, 1024), F32),
        vm((2, 2, 4, 512), jnp.int32),
        vm((2, 2, 4, 512), F32),
        vm((4, 512), jnp.int32),
        vm((4, 512), F32),
        vm((512, 1024), BF16),
        vm((1024, 512), BF16),
        vm((32, 32, 32), F32),
        vm((4, 2, 64, 128), BF16),
        vm((8, 64, 128), BF16),
        vm((8, 64, 128), BF16),
        vm((8, 64, 128), F32),
        vm((8, 64, 128), F32),
        vm((8, 64, 128), F32),
        vm((8, 2, 64, 128), BF16),
        vm((32, 16, 128), BF16),
        vm((32, 16, 128), BF16),
        vm((32, 512), BF16),
        vm((32, 2048), F32),
        vm((32, 2048), F32),
        vm((32, 2048), F32),
        vm((32, 2048), F32),
        vm((8, 32, 32), F32),
        vm((8, 32, 256), F32),
        vm((32, 2048), BF16),
        vm((32, 16, 128), BF16),
        vm((32, 16, 128), BF16),
        vm((8, 2, 16, 128), BF16),
        vm((512, 128), F32),
        vm((512, 128), F32),
        vm((512, 128), F32),
        vm((512, 128), BF16),
        vm((1024, 128), F32),
        vm((2, 2, 16, 8, 128), F32),
        vm((4, 8, 128), F32),
        vm((2, 128, 256), F32),
        vm((2, 128, 256), F32),
        vm((2, 128, 256), F32),
        vm((8, 64, 128), BF16),
        vm((ITERS - 1, 8, 64, 128), F32),
        vm((8, 64, 128), BF16),
        dma((9,)),
        dma((3,)),
        dma((3,)),
        dma((7,)),
        dma,
        dma((6,)),
        dma((2,)),
        dma((7,)),
        dma,
        dma((7,)),
        dma,
        dma,
        dma((4,)),
        dma,
        dma((4,)),
        dma((2, 2)),
        dma((2, 2)),
        dma((8,)),
        dma((ITERS,)),
    ]
    out = jax.ShapeDtypeStruct(right_side.shape, F32)
    return pl.pallas_call(
        kernel,
        out_shape=(out, out),
        in_specs=[pl.BlockSpec(memory_space=pl.ANY)] * 6,
        out_specs=(pl.BlockSpec(memory_space=pltpu.VMEM),) * 2,
        scratch_shapes=scratch,
        name="cg",
        compiler_params=pltpu.CompilerParams(
            collective_id=0, has_side_effects=True, vmem_limit_bytes=56 * 2**20
        ),
    )(right_side, spatial_basis, temporal_basis, spectral_weight.T, pierce_nodes, pierce_weights)


def solution(mesh):
    placed = (
        P("dir", "space", "tm"),
        P(),
        P(),
        P(None, ("space", "tm")),
        P("dir", "tm", None, None),
        P("dir", "tm", None, None),
    )
    return jax.shard_map(
        per_device,
        mesh=mesh,
        in_specs=placed,
        out_specs=(P("dir", "space", "tm"), P("dir", "space", "tm")),
        check_vma=False,
    )
```

```python
import jax
import jax.numpy as jnp
from jax import lax
from jax.experimental import pallas as pl
from jax.experimental.pallas import tpu as pltpu
from jax.sharding import PartitionSpec as P

ITERS = 4
MESH = pl.DeviceIdType.MESH
F32 = jnp.float32
BF16 = jnp.bfloat16


def hops(dy, dx):
    return min(dy, 4 - dy) + min(dx, 4 - dx)


CHIPS = sorted(((dy, dx) for dy in range(4) for dx in range(4)), key=lambda o: (hops(*o), o))
RANKS = [(dy, dc, dx) for dy, dx in CHIPS for dc in range(2)]
BACK = [RANKS.index((-dy % 4, dc, -dx % 4)) for dy, dc, dx in RANKS]
FAR_Z = (4, 3, 5, 2, 6, 1, 7)


def dot(a, b):
    return jnp.dot(a, b, preferred_element_type=F32)


def swap(a):
    flat = a.reshape(-1, 128)
    return pltpu.roll(flat, 64, 1).reshape(a.shape)


def fold(a):
    return jnp.sum(a.reshape(-1, 8, 128), axis=0)


def total(a):
    return jnp.sum(jnp.sum(a, axis=0, keepdims=True), axis=1, keepdims=True)


def kernel(
    rs_hbm, s_hbm, t_hbm, w_hbm, pn_hbm, pw_hbm,
    xo_ref, ro_ref,
    rs, sn, s4, st, tb, tt4, w_in, pn, pw, pnode, pwgt, g, gt,
    w_cols, isend, i1, i2, im, r, q, vb, fsend, frecv, ua, xv_, xm, xq, xd, wslot, wf, zb, bsend, brecv, vk,
    pr, pq, pd, pv_, pb, yacc, red, scal, xb, db, qb, osend, orecv, olast,
    load_sem, i1s, i1r, i2s, i2r, psend_sem, precv_sem, w1s, w1r, w2s, w2r,
    fs_sem, fr_sem, bs_sem, br_sem, rs_sem, rr_sem, os_sem, or_sem,
):
    z = lax.axis_index("space")
    m = lax.axis_index("tm")
    x = lax.axis_index("dir")
    y, core = m // 2, m % 2
    p = m * 4 + x
    left = lax.broadcasted_iota(jnp.int32, (1, 128), 1) < 64

    def dev(zz, mm, xx):
        return {"space": zz, "tm": mm, "dir": xx}

    def remote(src, dst, ss, rsem, to):
        return pltpu.make_async_remote_copy(
            src_ref=src, dst_ref=dst, send_sem=ss, recv_sem=rsem, device_id=to, device_id_type=MESH
        )

    loads = [
        pltpu.make_async_copy(rs_hbm, rs, load_sem.at[0]),
        pltpu.make_async_copy(pn_hbm, pn, load_sem.at[1]),
        pltpu.make_async_copy(pw_hbm, pw, load_sem.at[2]),
        pltpu.make_async_copy(w_hbm, w_in, load_sem.at[3]),
    ]
    s_load = pltpu.make_async_copy(s_hbm, sn, load_sem.at[4])

    def peer(j):
        dy, dc, dx = RANKS[j]
        return 2 * ((y + dy) % 4) + (core + dc) % 2, (x + dx) % 4

    def block(j):
        mm, xx = peer(j)
        return mm * 4 + xx

    for copy in loads + [s_load]:
        copy.start()
    for j in range(32):
        rows = pl.ds(pl.multiple_of(block(j) * 64, 64), 64)
        pltpu.make_async_copy(t_hbm.at[rows], tb.at[pl.ds(64 * j, 64)], load_sem.at[5]).start()

    barrier = pltpu.get_barrier_semaphore()

    def greet(to):
        pl.semaphore_signal(barrier, inc=1, device_id=to, device_id_type=MESH)

    for j in range(1, 32):
        greet(dev(z, *peer(j)))
    for o in range(2, 16):
        greet(dev((z + o // 2) % 8, 2 * y + (core + o) % 2, x))
    home = z // 2 == x
    for e in range(2):
        for dx in range(4):
            if dx == 0:
                @pl.when(z != 2 * x + e)
                def _():
                    greet(dev(2 * x + e, m, x))
            else:
                greet(dev(2 * x + e, m, (x + dx) % 4))
    for o in range(8):
        if o == 0:
            @pl.when(jnp.logical_not(home))
            def _():
                greet(dev(z, m, z // 2))
        else:
            greet(dev((z + o) % 8, m, z // 2))

    loads[0].wait()
    for h in range(2):
        for e in range(2):
            c = rs[e, :, 128 * h:128 * h + 128]
            top, bottom = c[:64], c[64:]
            isend[2 * h, e] = jnp.where(left, top, swap(bottom)).astype(BF16)
            isend[2 * h + 1, e] = jnp.where(left, swap(top), bottom).astype(BF16)
    i1[pl.ds(2 * x, 2)] = isend[x]
    for copy in loads[1:]:
        copy.wait()
    w_cols[...] = w_in[...].T.reshape(32, 32, 32)

    pl.semaphore_wait(barrier, 61 - 2 * home.astype(jnp.int32))

    for dx in (2, 1, 3):
        xx = (x + dx) % 4
        remote(isend.at[xx], i1.at[pl.ds(2 * x, 2)], i1s.at[dx - 1], i1r.at[dx - 1], dev(z, m, xx)).start()
    e_here = z % 2

    @pl.when(home)
    def _():
        for dx in range(1, 4):
            xx = (x + dx) % 4
            remote(pn.at[e_here, xx // 2], pnode, psend_sem.at[dx - 1], precv_sem.at[0], dev(z, m, xx)).start()
            remote(pw.at[e_here, xx // 2], pwgt, psend_sem.at[dx + 2], precv_sem.at[1], dev(z, m, xx)).start()
        pltpu.make_async_copy(pn.at[e_here, x // 2], pnode, precv_sem.at[0]).start()
        pltpu.make_async_copy(pw.at[e_here, x // 2], pwgt, precv_sem.at[1]).start()
    for o in range(1, 8):
        mm = (m + o) % 8
        remote(w_cols.at[mm * 4 + x], wslot.at[m], w1s.at[o - 1], w1r, dev(z, mm, x)).start()
    pltpu.make_async_copy(w_cols.at[p], wslot.at[m], w1r).start()

    def forward(xx):
        for e in range(2):
            zz = 2 * xx + e

            @pl.when(zz != z)
            def _():
                remote(i1.at[zz], i2.at[z], i2s.at[(zz + 7 - z) % 8], i2r, dev(zz, m, x)).start()

            @pl.when(zz == z)
            def _():
                pltpu.make_async_copy(i1.at[zz], i2.at[z], i2r).start()

    forward(x)
    s_load.wait()
    s4[...] = sn[...].T.reshape(4, 256, 1024)
    for j in range(32):
        own = block(j)
        st[32 * j:32 * j + 32, :] = s4[own // 8, pl.ds(pl.multiple_of(own % 8 * 32, 32), 32), :]
    for c in range(4):
        sn[:, 256 * c:256 * c + 256] = st[256 * c:256 * c + 256, :].T
    for dx in (1, 3, 2):
        xx = (x + 4 - dx) % 4
        span = i1.at[pl.ds(2 * xx, 2)]
        remote(span, span, i1s.at[dx - 1], i1r.at[dx - 1], dev(z, m, x)).wait_recv()
        forward(xx)

    pltpu.make_async_copy(wslot, wslot, w1r).wait()
    own_w = wf.at[z]
    for h in range(2):
        own_w[:, 128 * h:128 * h + 128] = jnp.concatenate([wslot[4 * h + i] for i in range(4)], axis=1)
    for o in FAR_Z:
        remote(wf.at[z], wf.at[z], w2s.at[o - 1], w2r, dev((z + o) % 8, m, x)).start()

    for ref in (r, q, xm, xq, xd, pr, pq, pd, xb, db, qb):
        ref[...] = jnp.zeros_like(ref)
    scal[0:2] = jnp.ones((2, 8, 128), F32)
    scal[2] = jnp.full((8, 128), -1.0, F32)
    scal[3] = jnp.zeros((8, 128), F32)

    pltpu.make_async_copy(pnode, pnode, precv_sem.at[0]).wait()
    pltpu.make_async_copy(pwgt, pwgt, precv_sem.at[1]).wait()
    nodes, wgts = pnode[...], pwgt[...]
    nodes_t = jnp.concatenate([nodes, nodes], axis=0).astype(F32).T.astype(jnp.int32)
    wgts_t = jnp.concatenate([wgts, wgts], axis=0).T
    for c in range(8):
        ids = lax.broadcasted_iota(jnp.int32, (128, 512), 0) + 128 * c
        acc = jnp.zeros((128, 512), F32)
        for j in range(4):
            acc += jnp.where(nodes[j:j + 1] == ids, wgts[j:j + 1], 0.0)
        gt[128 * c:128 * c + 128, :] = acc.astype(BF16)
        ids = lax.broadcasted_iota(jnp.int32, (512, 128), 1) + 128 * c
        acc = jnp.zeros((512, 128), F32)
        for j in range(4):
            acc += jnp.where(nodes_t[:, j:j + 1] == ids, wgts_t[:, j:j + 1], 0.0)
        g[:, 128 * c:128 * c + 128] = acc.astype(BF16)

    def transpose(c):
        @pl.loop(0, 8)
        def _(i):
            cols = pl.ds(pl.multiple_of(i * 256, 256), 256)
            tt4[c, cols, :] = tb[512 * c:512 * c + 512, cols].T

    pltpu.make_async_copy(t_hbm, tb, load_sem.at[5]).wait()
    for c in range(2, 4):
        transpose(c)

    pltpu.make_async_copy(i2, i2, i2r).wait()
    im[...] = i2[...].astype(F32)

    def reduce_start(par, step, value):
        own = (y * 4 + x, z * 2 + core)[step]
        slot = red.at[par, step, own]
        slot[...] = value
        if step == 0:
            where = [dev(z, 2 * ((y + dy) % 4) + core, (x + dx) % 4) for dy, dx in reversed(CHIPS[1:])]
        else:
            where = [dev((z + o) % 8, 2 * y + (core + dc) % 2, x) for o in FAR_Z for dc in range(2)]
            where.append(dev(z, 2 * y + 1 - core, x))
        for to in where:
            remote(slot, slot, rs_sem.at[par, step], rr_sem.at[par, step], to).start()

    def reduce_finish(par, step):
        span = red.at[par, step, pl.ds(0, 15)]
        both = remote(span, span, rs_sem.at[par, step], rr_sem.at[par, step], dev(z, m, x))
        both.wait_recv()
        both.wait_send()
        return jnp.sum(red[par, step], axis=0)

    def send_group(c, src, dst, ssem, rsem):
        for j in reversed(range(8 * c, 8 * c + 8)):
            if j > 0:
                remote(src.at[j], dst.at[BACK[j]], ssem, rsem.at[BACK[j] // 8], dev(z, *peer(j))).start()

    def wait_group(c, buf, rsem):
        span = buf.at[pl.ds(0, 7 if c == 0 else 8)]
        remote(span, span, rsem.at[c], rsem.at[c], dev(z, m, x)).wait_recv()

    def wait_sent(buf, ssem):
        span = buf.at[pl.ds(0, 31)]
        remote(span, span, ssem, ssem, dev(z, m, x)).wait_send()

    def scalars(j):
        sums = jnp.sum(reduce_finish(j % 2, 1), axis=1, keepdims=True)
        rr, ra, rb = sums[0:1], sums[1:2], sums[2:3]
        beta = jnp.where(j == 0, 0.0, rr / scal[0, 0:1, 0:1])
        curve = ra + beta * (2.0 * rb + beta * scal[1, 0:1, 0:1])
        for n, value in enumerate((rr, curve, rr / curve, beta)):
            scal[n] = jnp.broadcast_to(value, (8, 128))

    def factors():
        return scal[2, 0:1, 0:1], scal[3, 0:1, 0:1]

    slot_out = (z % 2) * 4 + x

    def ship(src, dst, sem):
        for o in FAR_Z + (0,):
            zz = (z + o) % 8

            def send():
                remote(src.at[zz], dst.at[slot_out], os_sem.at[o], sem, dev(zz, m, z // 2)).start()
            if o == 0:
                pl.when(jnp.logical_not(home))(send)

                @pl.when(home)
                def _():
                    pltpu.make_async_copy(src.at[zz], dst.at[slot_out], sem).start()
            else:
                send()

    def shipped(src, dst, sem):
        pltpu.make_async_copy(dst, dst, sem).wait()
        for o in range(8):
            if o == 0:
                @pl.when(jnp.logical_not(home))
                def _():
                    sent(src.at[0], os_sem.at[o])
            else:
                sent(src.at[0], os_sem.at[o])

    def sent(src, sem):
        remote(src, src, sem, sem, dev(z, m, x)).wait_send()

    def advance(tiles, x_out, r_out):
        alpha, beta = factors()
        for e in range(2):
            for h in range(2):
                a, b = tiles[4 * e + 2 * h].astype(F32), tiles[4 * e + 2 * h + 1].astype(F32)
                for part, rows in ((jnp.where(left, a, swap(b)), slice(0, 64)), (jnp.where(left, swap(a), b), slice(64, 128))):
                    at = (e, rows, slice(128 * h, 128 * h + 128))
                    qn = part + beta * qb[at]
                    dn = rs[at] + beta * db[at]
                    qb[at] = qn
                    db[at] = dn
                    x_out[at] = xb[at] + alpha * dn
                    r_out[at] = rs[at] - alpha * qn

    @pl.loop(0, ITERS)
    def _(it):
        par = it % 2
        v = im[...].reshape(512, 128)
        vsw = swap(v)
        vb[:, 0] = jnp.where(left, v, vsw).astype(BF16).reshape(8, 64, 128)
        vb[:, 1] = jnp.where(left, vsw, v).astype(BF16).reshape(8, 64, 128)
        vbv = vb[...].reshape(1024, 128)
        for c in (3, 2, 1, 0):
            u = dot(st[256 * c:256 * c + 256, :], vbv).reshape(8, 2, 16, 128)
            fsend[8 * c:8 * c + 8] = jnp.where(left, u[:, 0], u[:, 1]).astype(BF16)
            send_group(c, fsend, frecv, fs_sem, fr_sem)
        frecv[0] = fsend[0]

        @pl.when(it == 0)
        def _():
            for c in range(2):
                transpose(c)

        @pl.when(it > 0)
        def _():
            osend[...] = im[...].astype(BF16)
            ship(osend, orecv.at[it - 1], or_sem.at[it - 1])

        pv_[...] = dot(g[...], vbv)

        def modes(c):
            wait_group(c, frecv, fr_sem)
            tiles = frecv[8 * c:8 * c + 8].astype(F32)
            swapped = swap(tiles)
            for j in range(4):
                ua[0:16, 128 * j:128 * j + 128] = jnp.where(left, tiles[2 * j], swapped[2 * j + 1]).astype(BF16)
                ua[16:32, 128 * j:128 * j + 128] = jnp.where(left, swapped[2 * j], tiles[2 * j + 1]).astype(BF16)
            xv = dot(ua[...], tb[512 * c:512 * c + 512, :])
            if c == 0:
                xv_[...] = xv
            else:
                xv_[...] += xv

        modes(0)
        modes(1)

        @pl.when(it > 0)
        def _():
            scalars(it - 1)

        alpha, beta = factors()
        pold = pr[...] + beta * pd[...]
        pd[...] = pold
        pqn = pv_[...] + beta * pq[...]
        pq[...] = pqn
        pnew = pr[...] - alpha * pqn
        pr[...] = pnew
        pb[...] = pnew.astype(BF16)
        qn = v + beta * q[...].reshape(512, 128)
        q[...] = qn.reshape(8, 64, 128)
        rn = r[...].reshape(512, 128) - alpha * qn
        r[...] = rn.reshape(8, 64, 128)
        norm = fold(rn * rn)
        suma = 0.5 * fold(pnew * pnew)
        sumb = 0.5 * fold(pnew * pold)
        xd[...] = xm[...] + beta * xd[...]
        modes(2)
        modes(3)
        wait_sent(fsend, fs_sem)

        @pl.when(it == 0)
        def _():
            pltpu.make_async_copy(wf.at[pl.ds(0, 7)], wf.at[pl.ds(0, 7)], w2r).wait()

        for zz in range(8):
            cols = slice(256 * zz, 256 * zz + 256)
            xqn = xv_[:, cols] + beta * xq[:, cols]
            xq[:, cols] = xqn
            xn = xm[:, cols] - alpha * xqn
            xm[:, cols] = xn
            wx = wf[zz] * xn
            zb[:, cols] = wx.astype(BF16)
            qa, qc = wx * xn, wx * xd[:, cols]
            suma += fold(qa[:, :128] + qa[:, 128:])
            sumb += fold(qc[:, :128] + qc[:, 128:])
        row = lax.broadcasted_iota(jnp.int32, (8, 128), 0)
        one = [jnp.sum(part, axis=0, keepdims=True) for part in (norm, suma, sumb)]
        reduce_start(par, 0, jnp.where(row == 0, one[0], jnp.where(row == 1, one[1], one[2])))
        zv = zb[...]
        for c in (3, 2, 1, 0):
            w = dot(zv, tt4[c])
            for j in range(4):
                top, bottom = w[:16, 128 * j:128 * j + 128], w[16:, 128 * j:128 * j + 128]
                bsend[c * 8 + 2 * j] = jnp.where(left, top, swap(bottom)).astype(BF16)
                bsend[c * 8 + 2 * j + 1] = jnp.where(left, swap(top), bottom).astype(BF16)
            send_group(c, bsend, brecv, bs_sem, br_sem)
        brecv[0] = bsend[0]
        yacc[...] = dot(gt[...], pb[...])

        @pl.when(it > 0)
        def _():
            shipped(osend, orecv.at[it - 1], or_sem.at[it - 1])
            advance(orecv.at[it - 1], xb, rs)

        part = reduce_finish(par, 0)
        reduce_start(par, 1, part)
        for c in range(4):
            wait_group(c, brecv, br_sem)
            tiles = brecv[8 * c:8 * c + 8].astype(F32)
            swapped = swap(tiles)
            vk[:, 0] = jnp.where(left, tiles, swapped).astype(BF16)
            vk[:, 1] = jnp.where(left, swapped, tiles).astype(BF16)
            yacc[...] += dot(sn[:, 256 * c:256 * c + 256], vk[...].reshape(256, 128))
        wait_sent(bsend, bs_sem)
        ya = yacc[...].reshape(8, 2, 64, 128)
        im[...] = jnp.where(left, ya[:, 0], ya[:, 1])

    osend[...] = im[...].astype(BF16)
    ship(osend, olast, or_sem.at[ITERS - 1])
    scalars(ITERS - 1)

    for o in range(3):
        sent(isend.at[0], i1s.at[o])
    for o in range(7):
        sent(i1.at[0], i2s.at[o])

    @pl.when(home)
    def _():
        for dx in range(1, 4):
            sent(pn.at[0, 0], psend_sem.at[dx - 1])
            sent(pw.at[0, 0], psend_sem.at[dx + 2])
    for o in range(1, 8):
        sent(w_cols.at[0], w1s.at[o - 1])
        sent(wf.at[0], w2s.at[o - 1])

    shipped(osend, olast, or_sem.at[ITERS - 1])
    advance(olast, xo_ref, ro_ref)


def per_device(right_side, spatial_basis, temporal_basis, spectral_weight, pierce_nodes, pierce_weights):
    vm = pltpu.VMEM
    dma = pltpu.SemaphoreType.DMA
    scratch = [
        vm((2, 128, 256), F32),
        vm((1024, 1024), BF16),
        vm((4, 256, 1024), BF16),
        vm((1024, 1024), BF16),
        vm((2048, 2048), BF16),
        vm((4, 2048, 512), BF16),
        vm((32, 1024), F32),
        vm((2, 2, 4, 512), jnp.int32),
        vm((2, 2, 4, 512), F32),
        vm((4, 512), jnp.int32),
        vm((4, 512), F32),
        vm((512, 1024), BF16),
        vm((1024, 512), BF16),
        vm((32, 32, 32), F32),
        vm((4, 2, 64, 128), BF16),
        vm((8, 64, 128), BF16),
        vm((8, 64, 128), BF16),
        vm((8, 64, 128), F32),
        vm((8, 64, 128), F32),
        vm((8, 64, 128), F32),
        vm((8, 2, 64, 128), BF16),
        vm((32, 16, 128), BF16),
        vm((32, 16, 128), BF16),
        vm((32, 512), BF16),
        vm((32, 2048), F32),
        vm((32, 2048), F32),
        vm((32, 2048), F32),
        vm((32, 2048), F32),
        vm((8, 32, 32), F32),
        vm((8, 32, 256), F32),
        vm((32, 2048), BF16),
        vm((32, 16, 128), BF16),
        vm((32, 16, 128), BF16),
        vm((8, 2, 16, 128), BF16),
        vm((512, 128), F32),
        vm((512, 128), F32),
        vm((512, 128), F32),
        vm((512, 128), F32),
        vm((512, 128), BF16),
        vm((1024, 128), F32),
        vm((2, 2, 16, 8, 128), F32),
        vm((4, 8, 128), F32),
        vm((2, 128, 256), F32),
        vm((2, 128, 256), F32),
        vm((2, 128, 256), F32),
        vm((8, 64, 128), BF16),
        vm((ITERS - 1, 8, 64, 128), BF16),
        vm((8, 64, 128), BF16),
        dma((6,)),
        dma((3,)),
        dma((3,)),
        dma((7,)),
        dma,
        dma((6,)),
        dma((2,)),
        dma((7,)),
        dma,
        dma((7,)),
        dma,
        dma,
        dma((4,)),
        dma,
        dma((4,)),
        dma((2, 2)),
        dma((2, 2)),
        dma((8,)),
        dma((ITERS,)),
    ]
    out = jax.ShapeDtypeStruct(right_side.shape, F32)
    return pl.pallas_call(
        kernel,
        out_shape=(out, out),
        in_specs=[pl.BlockSpec(memory_space=pl.ANY)] * 6,
        out_specs=(pl.BlockSpec(memory_space=pltpu.VMEM),) * 2,
        scratch_shapes=scratch,
        name="cg",
        compiler_params=pltpu.CompilerParams(
            collective_id=0, has_side_effects=True, vmem_limit_bytes=56 * 2**20
        ),
    )(right_side, spatial_basis, temporal_basis, spectral_weight.T, pierce_nodes, pierce_weights)


def solution(mesh):
    placed = (
        P("dir", "space", "tm"),
        P(),
        P(),
        P(None, ("space", "tm")),
        P("dir", "tm", None, None),
        P("dir", "tm", None, None),
    )
    return jax.shard_map(
        per_device,
        mesh=mesh,
        in_specs=placed,
        out_specs=(P("dir", "space", "tm"), P("dir", "space", "tm")),
        check_vma=False,
    )
```

```python
import jax
import jax.numpy as jnp
from jax import lax
from jax.experimental import pallas as pl
from jax.experimental.pallas import tpu as pltpu
from jax.sharding import PartitionSpec as P

ITERS = 4
MESH = pl.DeviceIdType.MESH
F32 = jnp.float32
BF16 = jnp.bfloat16


def hops(dy, dx):
    return min(dy, 4 - dy) + min(dx, 4 - dx)


CHIPS = sorted(((dy, dx) for dy in range(4) for dx in range(4)), key=lambda o: (hops(*o), o))
RANKS = [(dy, dc, dx) for dy, dx in CHIPS for dc in range(2)]
BACK = [RANKS.index((-dy % 4, dc, -dx % 4)) for dy, dc, dx in RANKS]
FAR_Z = (4, 3, 5, 2, 6, 1, 7)
FWD_SEND, FWD_WAIT = ((24, 32), (16, 24), (8, 16), (0, 8)), ((0, 8), (8, 16), (16, 24), (24, 32))
BACK_SEND, BACK_WAIT = FWD_SEND, FWD_WAIT


def group_of(groups, rank):
    return [a <= rank < b for a, b in groups].index(True)


def dot(a, b):
    return jnp.dot(a, b, preferred_element_type=F32)


def swap(a):
    flat = a.reshape(-1, 128)
    return pltpu.roll(flat, 64, 1).reshape(a.shape)


def fold(a):
    return jnp.sum(a.reshape(-1, 8, 128), axis=0)


def total(a):
    return jnp.sum(jnp.sum(a, axis=0, keepdims=True), axis=1, keepdims=True)


def kernel(
    rs_hbm, s_hbm, t_hbm, w_hbm, pn_hbm, pw_hbm,
    xo_ref, ro_ref,
    rs, sn, s4, st, tb, tt, w_in, pn, pw, pnode, pwgt, g, gt,
    w_cols, isend, i1, i2, im, r, q, vb, fsend, frecv, ua, xv_, xm, xq, xd, wslot, wf, zb, bsend, brecv, vk,
    pr, pq, pd, pv_, pb, yacc, red, scal, xb, db, qb, osend, orecv, olast,
    load_sem, i1s, i1r, i2s, i2r, psend_sem, precv_sem, w1s, w1r, w2s, w2r,
    fs_sem, fr_sem, bs_sem, br_sem, rs_sem, rr_sem, os_sem, or_sem,
):
    z = lax.axis_index("space")
    m = lax.axis_index("tm")
    x = lax.axis_index("dir")
    y, core = m // 2, m % 2
    p = m * 4 + x
    left = lax.broadcasted_iota(jnp.int32, (1, 128), 1) < 64
    home = z // 2 == x

    def dev(zz, mm, xx):
        return {"space": zz, "tm": mm, "dir": xx}

    def remote(src, dst, ss, rsem, to):
        return pltpu.make_async_remote_copy(
            src_ref=src, dst_ref=dst, send_sem=ss, recv_sem=rsem, device_id=to, device_id_type=MESH
        )

    def peer(j):
        dy, dc, dx = RANKS[j]
        return 2 * ((y + dy) % 4) + (core + dc) % 2, (x + dx) % 4

    barrier = pltpu.get_barrier_semaphore()

    def greet(to):
        pl.semaphore_signal(barrier, inc=1, device_id=to, device_id_type=MESH)

    for o in FAR_Z:
        for dc in range(2):
            greet(dev((z + o) % 8, 2 * y + (core + dc) % 2, x))
    for j in reversed(range(1, 32)):
        greet(dev(z, *peer(j)))

    loads = [
        pltpu.make_async_copy(rs_hbm, rs, load_sem.at[0]),
        pltpu.make_async_copy(pn_hbm, pn, load_sem.at[1]),
        pltpu.make_async_copy(pw_hbm, pw, load_sem.at[2]),
        pltpu.make_async_copy(w_hbm, w_in, load_sem.at[3]),
    ]
    s_load = pltpu.make_async_copy(s_hbm, sn, load_sem.at[4])

    def block(j):
        mm, xx = peer(j)
        return mm * 4 + xx

    for copy in loads + [s_load]:
        copy.start()
    for j in range(32):
        rows = pl.ds(pl.multiple_of(block(j) * 64, 64), 64)
        pltpu.make_async_copy(t_hbm.at[rows], tb.at[pl.ds(64 * j, 64)], load_sem.at[5]).start()

    loads[0].wait()
    for h in range(2):
        for e in range(2):
            c = rs[e, :, 128 * h:128 * h + 128]
            top, bottom = c[:64], c[64:]
            isend[2 * h, e] = jnp.where(left, top, swap(bottom)).astype(BF16)
            isend[2 * h + 1, e] = jnp.where(left, swap(top), bottom).astype(BF16)
    i1[pl.ds(2 * x, 2)] = isend[x]
    for copy in loads[1:]:
        copy.wait()
    w_cols[...] = w_in[...].T.reshape(32, 32, 32)

    pl.semaphore_wait(barrier, 45)

    for dx in (2, 1, 3):
        xx = (x + dx) % 4
        remote(isend.at[xx], i1.at[pl.ds(2 * x, 2)], i1s.at[dx - 1], i1r.at[dx - 1], dev(z, m, xx)).start()
    e_here = z % 2

    @pl.when(home)
    def _():
        for dx in range(1, 4):
            xx = (x + dx) % 4
            remote(pn.at[e_here, xx // 2], pnode, psend_sem.at[dx - 1], precv_sem.at[0], dev(z, m, xx)).start()
            remote(pw.at[e_here, xx // 2], pwgt, psend_sem.at[dx + 2], precv_sem.at[1], dev(z, m, xx)).start()
        pltpu.make_async_copy(pn.at[e_here, x // 2], pnode, precv_sem.at[0]).start()
        pltpu.make_async_copy(pw.at[e_here, x // 2], pwgt, precv_sem.at[1]).start()
    for o in range(1, 8):
        mm = (m + o) % 8
        remote(w_cols.at[mm * 4 + x], wslot.at[m], w1s.at[o - 1], w1r, dev(z, mm, x)).start()
    pltpu.make_async_copy(w_cols.at[p], wslot.at[m], w1r).start()

    def forward(xx):
        for e in range(2):
            zz = 2 * xx + e

            @pl.when(zz != z)
            def _():
                remote(i1.at[zz], i2.at[z], i2s.at[(zz + 7 - z) % 8], i2r, dev(zz, m, x)).start()

            @pl.when(zz == z)
            def _():
                pltpu.make_async_copy(i1.at[zz], i2.at[z], i2r).start()

    forward(x)
    s_load.wait()
    s4[...] = sn[...].T.reshape(4, 256, 1024)
    for j in range(32):
        own = block(j)
        st[32 * j:32 * j + 32, :] = s4[own // 8, pl.ds(pl.multiple_of(own % 8 * 32, 32), 32), :]
    for c in range(4):
        sn[:, 256 * c:256 * c + 256] = st[256 * c:256 * c + 256, :].T
    for dx in (1, 3, 2):
        xx = (x + 4 - dx) % 4
        span = i1.at[pl.ds(2 * xx, 2)]
        remote(span, span, i1s.at[dx - 1], i1r.at[dx - 1], dev(z, m, x)).wait_recv()
        forward(xx)

    pltpu.make_async_copy(wslot, wslot, w1r).wait()
    own_w = wf.at[z]
    for h in range(2):
        own_w[:, 128 * h:128 * h + 128] = jnp.concatenate([wslot[4 * h + i] for i in range(4)], axis=1)
    for o in FAR_Z:
        remote(wf.at[z], wf.at[z], w2s.at[o - 1], w2r, dev((z + o) % 8, m, x)).start()

    for ref in (r, q, xm, xq, xd, pr, pq, pd, xb, db, qb):
        ref[...] = jnp.zeros_like(ref)
    scal[0:2] = jnp.ones((2, 8, 128), F32)
    scal[2] = jnp.full((8, 128), -1.0, F32)
    scal[3] = jnp.zeros((8, 128), F32)

    pltpu.make_async_copy(pnode, pnode, precv_sem.at[0]).wait()
    pltpu.make_async_copy(pwgt, pwgt, precv_sem.at[1]).wait()
    nodes, wgts = pnode[...], pwgt[...]
    nodes_t = jnp.concatenate([nodes, nodes], axis=0).astype(F32).T.astype(jnp.int32)
    wgts_t = jnp.concatenate([wgts, wgts], axis=0).T
    for c in range(8):
        ids = lax.broadcasted_iota(jnp.int32, (128, 512), 0) + 128 * c
        acc = jnp.zeros((128, 512), F32)
        for j in range(4):
            acc += jnp.where(nodes[j:j + 1] == ids, wgts[j:j + 1], 0.0)
        gt[128 * c:128 * c + 128, :] = acc.astype(BF16)
        ids = lax.broadcasted_iota(jnp.int32, (512, 128), 1) + 128 * c
        acc = jnp.zeros((512, 128), F32)
        for j in range(4):
            acc += jnp.where(nodes_t[:, j:j + 1] == ids, wgts_t[:, j:j + 1], 0.0)
        g[:, 128 * c:128 * c + 128] = acc.astype(BF16)

    def transpose(c):
        @pl.loop(0, 8)
        def _(i):
            cols = pl.ds(pl.multiple_of(i * 256, 256), 256)
            tt[cols, 512 * c:512 * c + 512] = tb[512 * c:512 * c + 512, cols].T

    pltpu.make_async_copy(t_hbm, tb, load_sem.at[5]).wait()
    for c in range(2, 4):
        transpose(c)

    pltpu.make_async_copy(i2, i2, i2r).wait()
    first = i2[...].astype(F32)
    turned = swap(first)
    im[...] = first
    vb[:, 0] = jnp.where(left, first, turned).astype(BF16)
    vb[:, 1] = jnp.where(left, turned, first).astype(BF16)

    def reduce_start(par, step, value):
        own = (y * 4 + x, z * 2 + core)[step]
        slot = red.at[par, step, own]
        slot[...] = value
        if step == 0:
            where = [dev(z, 2 * ((y + dy) % 4) + core, (x + dx) % 4) for dy, dx in reversed(CHIPS[1:])]
        else:
            where = [dev((z + o) % 8, 2 * y + (core + dc) % 2, x) for o in FAR_Z for dc in range(2)]
            where.append(dev(z, 2 * y + 1 - core, x))
        for to in where:
            remote(slot, slot, rs_sem.at[par, step], rr_sem.at[par, step], to).start()

    def reduce_finish(par, step):
        span = red.at[par, step, pl.ds(0, 15)]
        both = remote(span, span, rs_sem.at[par, step], rr_sem.at[par, step], dev(z, m, x))
        both.wait_recv()
        both.wait_send()
        return jnp.sum(red[par, step], axis=0)

    def send_group(ranks, groups, src, dst, ssem, rsem):
        for j in reversed(range(*ranks)):
            if j > 0:
                sem = rsem.at[group_of(groups, BACK[j])]
                remote(src.at[j], dst.at[BACK[j]], ssem, sem, dev(z, *peer(j))).start()

    def wait_group(ranks, groups, buf, rsem):
        a, b = ranks
        span = buf.at[pl.ds(0, b - max(a, 1))]
        sem = rsem.at[groups.index(ranks)]
        remote(span, span, sem, sem, dev(z, m, x)).wait_recv()

    def wait_sent(buf, ssem):
        span = buf.at[pl.ds(0, 31)]
        remote(span, span, ssem, ssem, dev(z, m, x)).wait_send()

    def scalars(j):
        sums = jnp.sum(reduce_finish(j % 2, 1), axis=1, keepdims=True)
        rr, ra, rb = sums[0:1], sums[1:2], sums[2:3]
        beta = jnp.where(j == 0, 0.0, rr / scal[0, 0:1, 0:1])
        curve = ra + beta * (2.0 * rb + beta * scal[1, 0:1, 0:1])
        for n, value in enumerate((rr, curve, rr / curve, beta)):
            scal[n] = jnp.broadcast_to(value, (8, 128))

    def factors():
        return scal[2, 0:1, 0:1], scal[3, 0:1, 0:1]

    slot_out = (z % 2) * 4 + x

    def ship(src, dst, sem):
        for o in FAR_Z + (0,):
            zz = (z + o) % 8

            def send():
                remote(src.at[zz], dst.at[slot_out], os_sem.at[o], sem, dev(zz, m, z // 2)).start()
            if o == 0:
                pl.when(jnp.logical_not(home))(send)

                @pl.when(home)
                def _():
                    pltpu.make_async_copy(src.at[zz], dst.at[slot_out], sem).start()
            else:
                send()

    def shipped(src, dst, sem):
        pltpu.make_async_copy(dst, dst, sem).wait()
        for o in range(8):
            if o == 0:
                @pl.when(jnp.logical_not(home))
                def _():
                    sent(src.at[0], os_sem.at[o])
            else:
                sent(src.at[0], os_sem.at[o])

    def sent(src, sem):
        remote(src, src, sem, sem, dev(z, m, x)).wait_send()

    def advance(tiles, x_out, r_out):
        alpha, beta = factors()
        for e in range(2):
            for h in range(2):
                a, b = tiles[4 * e + 2 * h].astype(F32), tiles[4 * e + 2 * h + 1].astype(F32)
                for part, rows in ((jnp.where(left, a, swap(b)), slice(0, 64)), (jnp.where(left, swap(a), b), slice(64, 128))):
                    at = (e, rows, slice(128 * h, 128 * h + 128))
                    qn = part + beta * qb[at]
                    dn = rs[at] + beta * db[at]
                    qb[at] = qn
                    db[at] = dn
                    x_out[at] = xb[at] + alpha * dn
                    r_out[at] = rs[at] - alpha * qn

    @pl.loop(0, ITERS)
    def _(it):
        par = it % 2
        vbv = vb[...].reshape(1024, 128)
        for a, b in FWD_SEND:
            u = dot(st[32 * a:32 * b, :], vbv).reshape(b - a, 2, 16, 128)
            fsend[a:b] = jnp.where(left, u[:, 0], u[:, 1]).astype(BF16)
            send_group((a, b), FWD_WAIT, fsend, frecv, fs_sem, fr_sem)
        frecv[0] = fsend[0]

        @pl.when(it == 0)
        def _():
            for c in range(2):
                transpose(c)

        @pl.when(it > 0)
        def _():
            osend[...] = im[...].astype(BF16)
            ship(osend, orecv.at[it - 1], or_sem.at[it - 1])

        pv_[...] = dot(g[...], vbv)
        v = im[...].reshape(512, 128)

        def modes(ranks):
            a, b = ranks
            wait_group(ranks, FWD_WAIT, frecv, fr_sem)
            tiles = frecv[a:b].astype(F32)
            swapped = swap(tiles)
            for j in range((b - a) // 2):
                ua[0:16, 128 * j:128 * j + 128] = jnp.where(left, tiles[2 * j], swapped[2 * j + 1]).astype(BF16)
                ua[16:32, 128 * j:128 * j + 128] = jnp.where(left, swapped[2 * j], tiles[2 * j + 1]).astype(BF16)
            xv = dot(ua[:, :64 * (b - a)], tb[64 * a:64 * b, :])
            if ranks == FWD_WAIT[0]:
                xv_[...] = xv
            else:
                xv_[...] += xv

        for ranks in FWD_WAIT[:-1]:
            modes(ranks)

        @pl.when(it > 0)
        def _():
            scalars(it - 1)

        alpha, beta = factors()
        pold = pr[...] + beta * pd[...]
        pd[...] = pold
        pqn = pv_[...] + beta * pq[...]
        pq[...] = pqn
        pnew = pr[...] - alpha * pqn
        pr[...] = pnew
        pb[...] = pnew.astype(BF16)
        qn = v + beta * q[...].reshape(512, 128)
        q[...] = qn.reshape(8, 64, 128)
        rn = r[...].reshape(512, 128) - alpha * qn
        r[...] = rn.reshape(8, 64, 128)
        norm = fold(rn * rn)
        suma = 0.5 * fold(pnew * pnew)
        sumb = 0.5 * fold(pnew * pold)
        xd[...] = xm[...] + beta * xd[...]
        modes(FWD_WAIT[-1])
        wait_sent(fsend, fs_sem)

        @pl.when(it == 0)
        def _():
            pltpu.make_async_copy(wf.at[pl.ds(0, 7)], wf.at[pl.ds(0, 7)], w2r).wait()

        for zz in range(8):
            cols = slice(256 * zz, 256 * zz + 256)
            xqn = xv_[:, cols] + beta * xq[:, cols]
            xq[:, cols] = xqn
            xn = xm[:, cols] - alpha * xqn
            xm[:, cols] = xn
            wx = wf[zz] * xn
            zb[:, cols] = wx.astype(BF16)
            qa, qc = wx * xn, wx * xd[:, cols]
            suma += fold(qa[:, :128] + qa[:, 128:])
            sumb += fold(qc[:, :128] + qc[:, 128:])
        row = lax.broadcasted_iota(jnp.int32, (8, 128), 0)
        one = [jnp.sum(part, axis=0, keepdims=True) for part in (norm, suma, sumb)]
        reduce_start(par, 0, jnp.where(row == 0, one[0], jnp.where(row == 1, one[1], one[2])))
        zv = zb[...]
        for a, b in BACK_SEND:
            w = dot(zv, tt[:, 64 * a:64 * b])
            for j in range((b - a) // 2):
                top, bottom = w[:16, 128 * j:128 * j + 128], w[16:, 128 * j:128 * j + 128]
                bsend[a + 2 * j] = jnp.where(left, top, swap(bottom)).astype(BF16)
                bsend[a + 2 * j + 1] = jnp.where(left, swap(top), bottom).astype(BF16)
            send_group((a, b), BACK_WAIT, bsend, brecv, bs_sem, br_sem)
        brecv[0] = bsend[0]
        yacc[...] = dot(gt[...], pb[...])

        @pl.when(it > 0)
        def _():
            shipped(osend, orecv.at[it - 1], or_sem.at[it - 1])
            advance(orecv.at[it - 1], xb, rs)

        part = reduce_finish(par, 0)
        reduce_start(par, 1, part)
        for ranks in BACK_WAIT:
            a, b = ranks
            wait_group(ranks, BACK_WAIT, brecv, br_sem)
            tiles = brecv[a:b].astype(F32)
            swapped = swap(tiles)
            vk[a:b, 0] = jnp.where(left, tiles, swapped).astype(BF16)
            vk[a:b, 1] = jnp.where(left, swapped, tiles).astype(BF16)
            part = yacc[...] + dot(sn[:, 32 * a:32 * b], vk[a:b].reshape(32 * (b - a), 128))
            if ranks != BACK_WAIT[-1]:
                yacc[...] = part
        wait_sent(bsend, bs_sem)
        ya = part.reshape(8, 2, 64, 128)
        vb[...] = ya.astype(BF16)
        im[...] = jnp.where(left, ya[:, 0], ya[:, 1])

    osend[...] = im[...].astype(BF16)
    ship(osend, olast, or_sem.at[ITERS - 1])
    scalars(ITERS - 1)

    for o in range(3):
        sent(isend.at[0], i1s.at[o])
    for o in range(7):
        sent(i1.at[0], i2s.at[o])

    @pl.when(home)
    def _():
        for dx in range(1, 4):
            sent(pn.at[0, 0], psend_sem.at[dx - 1])
            sent(pw.at[0, 0], psend_sem.at[dx + 2])
    for o in range(1, 8):
        sent(w_cols.at[0], w1s.at[o - 1])
        sent(wf.at[0], w2s.at[o - 1])

    shipped(osend, olast, or_sem.at[ITERS - 1])
    advance(olast, xo_ref, ro_ref)


def hand_over(x_in, r_in, x_out, r_out):
    x_out[...] = x_in[...]
    r_out[...] = r_in[...]


def per_device(right_side, spatial_basis, temporal_basis, spectral_weight, pierce_nodes, pierce_weights):
    vm = pltpu.VMEM
    dma = pltpu.SemaphoreType.DMA
    scratch = [
        vm((2, 128, 256), F32),
        vm((1024, 1024), BF16),
        vm((4, 256, 1024), BF16),
        vm((1024, 1024), BF16),
        vm((2048, 2048), BF16),
        vm((2048, 2048), BF16),
        vm((32, 1024), F32),
        vm((2, 2, 4, 512), jnp.int32),
        vm((2, 2, 4, 512), F32),
        vm((4, 512), jnp.int32),
        vm((4, 512), F32),
        vm((512, 1024), BF16),
        vm((1024, 512), BF16),
        vm((32, 32, 32), F32),
        vm((4, 2, 64, 128), BF16),
        vm((8, 64, 128), BF16),
        vm((8, 64, 128), BF16),
        vm((8, 64, 128), F32),
        vm((8, 64, 128), F32),
        vm((8, 64, 128), F32),
        vm((8, 2, 64, 128), BF16),
        vm((32, 16, 128), BF16),
        vm((32, 16, 128), BF16),
        vm((32, 2048), BF16),
        vm((32, 2048), F32),
        vm((32, 2048), F32),
        vm((32, 2048), F32),
        vm((32, 2048), F32),
        vm((8, 32, 32), F32),
        vm((8, 32, 256), F32),
        vm((32, 2048), BF16),
        vm((32, 16, 128), BF16),
        vm((32, 16, 128), BF16),
        vm((32, 2, 16, 128), BF16),
        vm((512, 128), F32),
        vm((512, 128), F32),
        vm((512, 128), F32),
        vm((512, 128), F32),
        vm((512, 128), BF16),
        vm((1024, 128), F32),
        vm((2, 2, 16, 8, 128), F32),
        vm((4, 8, 128), F32),
        vm((2, 128, 256), F32),
        vm((2, 128, 256), F32),
        vm((2, 128, 256), F32),
        vm((8, 64, 128), BF16),
        vm((ITERS - 1, 8, 64, 128), BF16),
        vm((8, 64, 128), BF16),
        dma((6,)),
        dma((3,)),
        dma((3,)),
        dma((7,)),
        dma,
        dma((6,)),
        dma((2,)),
        dma((7,)),
        dma,
        dma((7,)),
        dma,
        dma,
        dma((4,)),
        dma,
        dma((4,)),
        dma((2, 2)),
        dma((2, 2)),
        dma((8,)),
        dma((ITERS,)),
    ]
    out = jax.ShapeDtypeStruct(right_side.shape, F32)
    results = pl.pallas_call(
        kernel,
        out_shape=(out, out),
        in_specs=[pl.BlockSpec(memory_space=pl.ANY)] * 6,
        out_specs=(pl.BlockSpec(memory_space=pltpu.VMEM),) * 2,
        scratch_shapes=scratch,
        name="cg",
        compiler_params=pltpu.CompilerParams(
            collective_id=0, has_side_effects=True, vmem_limit_bytes=56 * 2**20
        ),
    )(right_side, spatial_basis, temporal_basis, spectral_weight.T, pierce_nodes, pierce_weights)
    whole = (pl.BlockSpec(memory_space=vm),) * 2
    return pl.pallas_call(
        hand_over,
        out_shape=(out, out),
        in_specs=whole,
        out_specs=whole,
        name="hand_over",
    )(*results)


def solution(mesh):
    placed = (
        P("dir", "space", "tm"),
        P(),
        P(),
        P(None, ("space", "tm")),
        P("dir", "tm", None, None),
        P("dir", "tm", None, None),
    )
    return jax.shard_map(
        per_device,
        mesh=mesh,
        in_specs=placed,
        out_specs=(P("dir", "space", "tm"), P("dir", "space", "tm")),
        check_vma=False,
    )
```

```python
import jax
import jax.numpy as jnp
from jax import lax
from jax.experimental import pallas as pl
from jax.experimental.pallas import tpu as pltpu
from jax.sharding import PartitionSpec as P

ITERS = 4
MESH = pl.DeviceIdType.MESH
F32 = jnp.float32
BF16 = jnp.bfloat16


def hops(dy, dx):
    return min(dy, 4 - dy) + min(dx, 4 - dx)


CHIPS = sorted(((dy, dx) for dy in range(4) for dx in range(4)), key=lambda o: (hops(*o), o))
RANKS = [(dy, dc, dx) for dy, dx in CHIPS for dc in range(2)]
BACK = [RANKS.index((-dy % 4, dc, -dx % 4)) for dy, dc, dx in RANKS]
FAR_Z = (4, 3, 5, 2, 6, 1, 7)
FWD_SEND, FWD_WAIT = ((24, 32), (16, 24), (8, 16), (0, 8)), ((0, 8), (8, 16), (16, 24), (24, 32))
BACK_SEND, BACK_WAIT = FWD_SEND, FWD_WAIT


def group_of(groups, rank):
    return [a <= rank < b for a, b in groups].index(True)


def dot(a, b):
    return jnp.dot(a, b, preferred_element_type=F32)


def swap(a):
    flat = a.reshape(-1, 128)
    return pltpu.roll(flat, 64, 1).reshape(a.shape)


def fold(a):
    return jnp.sum(a.reshape(-1, 8, 128), axis=0)


def total(a):
    return jnp.sum(jnp.sum(a, axis=0, keepdims=True), axis=1, keepdims=True)


def kernel(
    rs_hbm, s_hbm, t_hbm, w_hbm, pn_hbm, pw_hbm,
    xo_ref, ro_ref,
    rs, sn, s4, st, tb, tt, w_in, pn, pw, pnode, pwgt, g, gt,
    w_cols, isend, i1, i2, im, r, q, vb, fsend, frecv, ua, xv_, xm, xq, xd, wslot, wf, zb, bsend, brecv, vk,
    pr, pq, pd, pv_, pb, yacc, red, scal, xb, db, qb, osend, orecv, olast,
    load_sem, i1s, i1r, i2s, i2r, psend_sem, precv_sem, w1s, w1r, w2s, w2r,
    fs_sem, fr_sem, bs_sem, br_sem, rs_sem, rr_sem, os_sem, or_sem,
):
    z = lax.axis_index("space")
    m = lax.axis_index("tm")
    x = lax.axis_index("dir")
    y, core = m // 2, m % 2
    p = m * 4 + x
    left = lax.broadcasted_iota(jnp.int32, (1, 128), 1) < 64
    home = z // 2 == x

    def dev(zz, mm, xx):
        return {"space": zz, "tm": mm, "dir": xx}

    def remote(src, dst, ss, rsem, to):
        return pltpu.make_async_remote_copy(
            src_ref=src, dst_ref=dst, send_sem=ss, recv_sem=rsem, device_id=to, device_id_type=MESH
        )

    def peer(j):
        dy, dc, dx = RANKS[j]
        return 2 * ((y + dy) % 4) + (core + dc) % 2, (x + dx) % 4

    barrier = pltpu.get_barrier_semaphore()

    def greet(to):
        pl.semaphore_signal(barrier, inc=1, device_id=to, device_id_type=MESH)

    for o in FAR_Z:
        for dc in range(2):
            greet(dev((z + o) % 8, 2 * y + (core + dc) % 2, x))
    for j in reversed(range(1, 32)):
        greet(dev(z, *peer(j)))

    loads = [
        pltpu.make_async_copy(rs_hbm, rs, load_sem.at[0]),
        pltpu.make_async_copy(pn_hbm, pn, load_sem.at[1]),
        pltpu.make_async_copy(pw_hbm, pw, load_sem.at[2]),
        pltpu.make_async_copy(w_hbm, w_in, load_sem.at[3]),
    ]
    s_load = pltpu.make_async_copy(s_hbm, sn, load_sem.at[4])

    def block(j):
        mm, xx = peer(j)
        return mm * 4 + xx

    for copy in loads + [s_load]:
        copy.start()
    for j in range(32):
        rows = pl.ds(pl.multiple_of(block(j) * 64, 64), 64)
        pltpu.make_async_copy(t_hbm.at[rows], tb.at[pl.ds(64 * j, 64)], load_sem.at[5]).start()

    loads[0].wait()
    for h in range(2):
        for e in range(2):
            c = rs[e, :, 128 * h:128 * h + 128]
            top, bottom = c[:64], c[64:]
            isend[2 * h, e] = jnp.where(left, top, swap(bottom)).astype(BF16)
            isend[2 * h + 1, e] = jnp.where(left, swap(top), bottom).astype(BF16)
    i1[pl.ds(2 * x, 2)] = isend[x]
    for copy in loads[1:]:
        copy.wait()
    w_cols[...] = w_in[...].T.reshape(32, 32, 32)

    pl.semaphore_wait(barrier, 45)

    for dx in (2, 1, 3):
        xx = (x + dx) % 4
        remote(isend.at[xx], i1.at[pl.ds(2 * x, 2)], i1s.at[dx - 1], i1r.at[dx - 1], dev(z, m, xx)).start()
    e_here = z % 2

    @pl.when(home)
    def _():
        for dx in range(1, 4):
            xx = (x + dx) % 4
            remote(pn.at[e_here, xx // 2], pnode, psend_sem.at[dx - 1], precv_sem.at[0], dev(z, m, xx)).start()
            remote(pw.at[e_here, xx // 2], pwgt, psend_sem.at[dx + 2], precv_sem.at[1], dev(z, m, xx)).start()
        pltpu.make_async_copy(pn.at[e_here, x // 2], pnode, precv_sem.at[0]).start()
        pltpu.make_async_copy(pw.at[e_here, x // 2], pwgt, precv_sem.at[1]).start()
    for o in range(1, 8):
        mm = (m + o) % 8
        remote(w_cols.at[mm * 4 + x], wslot.at[m], w1s.at[o - 1], w1r, dev(z, mm, x)).start()
    pltpu.make_async_copy(w_cols.at[p], wslot.at[m], w1r).start()

    def forward(xx):
        for e in range(2):
            zz = 2 * xx + e

            @pl.when(zz != z)
            def _():
                remote(i1.at[zz], i2.at[z], i2s.at[(zz + 7 - z) % 8], i2r, dev(zz, m, x)).start()

            @pl.when(zz == z)
            def _():
                pltpu.make_async_copy(i1.at[zz], i2.at[z], i2r).start()

    forward(x)
    s_load.wait()
    s4[...] = sn[...].T.reshape(4, 256, 1024)
    for j in range(32):
        own = block(j)
        st[32 * j:32 * j + 32, :] = s4[own // 8, pl.ds(pl.multiple_of(own % 8 * 32, 32), 32), :]
    for c in range(4):
        sn[:, 256 * c:256 * c + 256] = st[256 * c:256 * c + 256, :].T
    for dx in (1, 3, 2):
        xx = (x + 4 - dx) % 4
        span = i1.at[pl.ds(2 * xx, 2)]
        remote(span, span, i1s.at[dx - 1], i1r.at[dx - 1], dev(z, m, x)).wait_recv()
        forward(xx)

    pltpu.make_async_copy(wslot, wslot, w1r).wait()
    own_w = wf.at[z]
    for h in range(2):
        own_w[:, 128 * h:128 * h + 128] = jnp.concatenate([wslot[4 * h + i] for i in range(4)], axis=1)
    for o in FAR_Z:
        remote(wf.at[z], wf.at[z], w2s.at[o - 1], w2r, dev((z + o) % 8, m, x)).start()

    for ref in (r, q, xm, xq, xd, pr, pq, pd, xb, db, qb):
        ref[...] = jnp.zeros_like(ref)
    scal[0:2] = jnp.ones((2, 8, 128), F32)
    scal[2] = jnp.full((8, 128), -1.0, F32)
    scal[3] = jnp.zeros((8, 128), F32)

    pltpu.make_async_copy(pnode, pnode, precv_sem.at[0]).wait()
    pltpu.make_async_copy(pwgt, pwgt, precv_sem.at[1]).wait()
    nodes, wgts = pnode[...], pwgt[...]
    nodes_t = jnp.concatenate([nodes, nodes], axis=0).astype(F32).T.astype(jnp.int32)
    wgts_t = jnp.concatenate([wgts, wgts], axis=0).T
    for c in range(8):
        ids = lax.broadcasted_iota(jnp.int32, (128, 512), 0) + 128 * c
        acc = jnp.zeros((128, 512), F32)
        for j in range(4):
            acc += jnp.where(nodes[j:j + 1] == ids, wgts[j:j + 1], 0.0)
        gt[128 * c:128 * c + 128, :] = acc.astype(BF16)
        ids = lax.broadcasted_iota(jnp.int32, (512, 128), 1) + 128 * c
        acc = jnp.zeros((512, 128), F32)
        for j in range(4):
            acc += jnp.where(nodes_t[:, j:j + 1] == ids, wgts_t[:, j:j + 1], 0.0)
        g[:, 128 * c:128 * c + 128] = acc.astype(BF16)

    def transpose(c):
        @pl.loop(0, 8)
        def _(i):
            cols = pl.ds(pl.multiple_of(i * 256, 256), 256)
            tt[cols, 512 * c:512 * c + 512] = tb[512 * c:512 * c + 512, cols].T

    pltpu.make_async_copy(t_hbm, tb, load_sem.at[5]).wait()
    for c in range(2, 4):
        transpose(c)

    pltpu.make_async_copy(i2, i2, i2r).wait()
    first = i2[...].astype(F32)
    turned = swap(first)
    im[...] = first
    vb[:, 0] = jnp.where(left, first, turned).astype(BF16)
    vb[:, 1] = jnp.where(left, turned, first).astype(BF16)

    def reduce_start(par, step, value):
        own = (y * 4 + x, z * 2 + core)[step]
        slot = red.at[par, step, own]
        slot[...] = value
        if step == 0:
            where = [dev(z, 2 * ((y + dy) % 4) + core, (x + dx) % 4) for dy, dx in reversed(CHIPS[1:])]
        else:
            where = [dev((z + o) % 8, 2 * y + (core + dc) % 2, x) for o in FAR_Z for dc in range(2)]
            where.append(dev(z, 2 * y + 1 - core, x))
        for to in where:
            remote(slot, slot, rs_sem.at[par, step], rr_sem.at[par, step], to).start()

    def reduce_finish(par, step):
        span = red.at[par, step, pl.ds(0, 15)]
        both = remote(span, span, rs_sem.at[par, step], rr_sem.at[par, step], dev(z, m, x))
        both.wait_recv()
        both.wait_send()
        return jnp.sum(red[par, step], axis=0)

    def send_group(ranks, groups, src, dst, ssem, rsem):
        for j in reversed(range(*ranks)):
            if j > 0:
                sem = rsem.at[group_of(groups, BACK[j])]
                remote(src.at[j], dst.at[BACK[j]], ssem, sem, dev(z, *peer(j))).start()

    def wait_group(ranks, groups, buf, rsem):
        a, b = ranks
        span = buf.at[pl.ds(0, b - max(a, 1))]
        sem = rsem.at[groups.index(ranks)]
        remote(span, span, sem, sem, dev(z, m, x)).wait_recv()

    def wait_sent(buf, ssem):
        span = buf.at[pl.ds(0, 31)]
        remote(span, span, ssem, ssem, dev(z, m, x)).wait_send()

    def scalars(j):
        sums = jnp.sum(reduce_finish(j % 2, 1), axis=1, keepdims=True)
        rr, ra, rb = sums[0:1], sums[1:2], sums[2:3]
        beta = jnp.where(j == 0, 0.0, rr / scal[0, 0:1, 0:1])
        curve = ra + beta * (2.0 * rb + beta * scal[1, 0:1, 0:1])
        for n, value in enumerate((rr, curve, rr / curve, beta)):
            scal[n] = jnp.broadcast_to(value, (8, 128))

    def factors():
        return scal[2, 0:1, 0:1], scal[3, 0:1, 0:1]

    slot_out = (z % 2) * 4 + x

    def ship(src, dst, sem):
        for o in FAR_Z + (0,):
            zz = (z + o) % 8

            def send():
                remote(src.at[zz], dst.at[slot_out], os_sem.at[o], sem, dev(zz, m, z // 2)).start()
            if o == 0:
                pl.when(jnp.logical_not(home))(send)

                @pl.when(home)
                def _():
                    pltpu.make_async_copy(src.at[zz], dst.at[slot_out], sem).start()
            else:
                send()

    def shipped(src, dst, sem):
        pltpu.make_async_copy(dst, dst, sem).wait()
        for o in range(8):
            if o == 0:
                @pl.when(jnp.logical_not(home))
                def _():
                    sent(src.at[0], os_sem.at[o])
            else:
                sent(src.at[0], os_sem.at[o])

    def sent(src, sem):
        remote(src, src, sem, sem, dev(z, m, x)).wait_send()

    def advance(tiles):
        alpha, beta = factors()
        for e in range(2):
            for h in range(2):
                a, b = tiles[4 * e + 2 * h].astype(F32), tiles[4 * e + 2 * h + 1].astype(F32)
                for part, rows in ((jnp.where(left, a, swap(b)), slice(0, 64)), (jnp.where(left, swap(a), b), slice(64, 128))):
                    at = (e, rows, slice(128 * h, 128 * h + 128))
                    qn = part + beta * qb[at]
                    dn = rs[at] + beta * db[at]
                    qb[at] = qn
                    db[at] = dn
                    xb[at] += alpha * dn
                    rs[at] -= alpha * qn

    @pl.loop(0, ITERS)
    def _(it):
        par = it % 2
        vbv = vb[...].reshape(1024, 128)
        for a, b in FWD_SEND:
            u = dot(st[32 * a:32 * b, :], vbv).reshape(b - a, 2, 16, 128)
            fsend[a:b] = jnp.where(left, u[:, 0], u[:, 1]).astype(BF16)
            send_group((a, b), FWD_WAIT, fsend, frecv, fs_sem, fr_sem)
        frecv[0] = fsend[0]

        @pl.when(it == 0)
        def _():
            for c in range(2):
                transpose(c)

        @pl.when(it > 0)
        def _():
            osend[...] = im[...].astype(BF16)
            ship(osend, orecv.at[it - 1], or_sem.at[it - 1])

        pv_[...] = dot(g[...], vbv)
        v = im[...].reshape(512, 128)

        def modes(ranks):
            a, b = ranks
            wait_group(ranks, FWD_WAIT, frecv, fr_sem)
            tiles = frecv[a:b].astype(F32)
            swapped = swap(tiles)
            for j in range((b - a) // 2):
                ua[0:16, 128 * j:128 * j + 128] = jnp.where(left, tiles[2 * j], swapped[2 * j + 1]).astype(BF16)
                ua[16:32, 128 * j:128 * j + 128] = jnp.where(left, swapped[2 * j], tiles[2 * j + 1]).astype(BF16)
            xv = dot(ua[:, :64 * (b - a)], tb[64 * a:64 * b, :])
            if ranks == FWD_WAIT[0]:
                xv_[...] = xv
            else:
                xv_[...] += xv

        @pl.when(it > 0)
        def _():
            scalars(it - 1)

        alpha, beta = factors()
        pold = pr[...] + beta * pd[...]
        pd[...] = pold
        pqn = pv_[...] + beta * pq[...]
        pq[...] = pqn
        pnew = pr[...] - alpha * pqn
        pr[...] = pnew
        pb[...] = pnew.astype(BF16)
        qn = v + beta * q[...].reshape(512, 128)
        q[...] = qn.reshape(8, 64, 128)
        rn = r[...].reshape(512, 128) - alpha * qn
        r[...] = rn.reshape(8, 64, 128)
        norm = fold(rn * rn)
        suma = 0.5 * fold(pnew * pnew)
        sumb = 0.5 * fold(pnew * pold)
        xd[...] = xm[...] + beta * xd[...]
        for ranks in FWD_WAIT:
            modes(ranks)
        wait_sent(fsend, fs_sem)

        @pl.when(it == 0)
        def _():
            pltpu.make_async_copy(wf.at[pl.ds(0, 7)], wf.at[pl.ds(0, 7)], w2r).wait()

        for zz in range(8):
            cols = slice(256 * zz, 256 * zz + 256)
            xqn = xv_[:, cols] + beta * xq[:, cols]
            xq[:, cols] = xqn
            xn = xm[:, cols] - alpha * xqn
            xm[:, cols] = xn
            wx = wf[zz] * xn
            zb[:, cols] = wx.astype(BF16)
            qa, qc = wx * xn, wx * xd[:, cols]
            suma += fold(qa[:, :128] + qa[:, 128:])
            sumb += fold(qc[:, :128] + qc[:, 128:])
        row = lax.broadcasted_iota(jnp.int32, (8, 128), 0)
        one = [jnp.sum(part, axis=0, keepdims=True) for part in (norm, suma, sumb)]
        reduce_start(par, 0, jnp.where(row == 0, one[0], jnp.where(row == 1, one[1], one[2])))
        zv = zb[...]
        for a, b in BACK_SEND:
            w = dot(zv, tt[:, 64 * a:64 * b])
            for j in range((b - a) // 2):
                top, bottom = w[:16, 128 * j:128 * j + 128], w[16:, 128 * j:128 * j + 128]
                bsend[a + 2 * j] = jnp.where(left, top, swap(bottom)).astype(BF16)
                bsend[a + 2 * j + 1] = jnp.where(left, swap(top), bottom).astype(BF16)
            send_group((a, b), BACK_WAIT, bsend, brecv, bs_sem, br_sem)
        brecv[0] = bsend[0]
        yacc[...] = dot(gt[...], pb[...])

        @pl.when(it > 0)
        def _():
            shipped(osend, orecv.at[it - 1], or_sem.at[it - 1])
            advance(orecv.at[it - 1])

        part = reduce_finish(par, 0)
        reduce_start(par, 1, part)
        for ranks in BACK_WAIT:
            a, b = ranks
            wait_group(ranks, BACK_WAIT, brecv, br_sem)
            tiles = brecv[a:b].astype(F32)
            swapped = swap(tiles)
            vk[a:b, 0] = jnp.where(left, tiles, swapped).astype(BF16)
            vk[a:b, 1] = jnp.where(left, swapped, tiles).astype(BF16)
            part = yacc[...] + dot(sn[:, 32 * a:32 * b], vk[a:b].reshape(32 * (b - a), 128))
            if ranks != BACK_WAIT[-1]:
                yacc[...] = part
        wait_sent(bsend, bs_sem)
        ya = part.reshape(8, 2, 64, 128)
        vb[...] = ya.astype(BF16)
        im[...] = jnp.where(left, ya[:, 0], ya[:, 1])

    osend[...] = im[...].astype(BF16)
    ship(osend, olast, or_sem.at[ITERS - 1])
    scalars(ITERS - 1)
    alpha, beta = factors()
    xo_ref[...] = xb[...] + alpha * (rs[...] + beta * db[...])
    rs[...] = rs[...] - (alpha * beta) * qb[...]

    for o in range(3):
        sent(isend.at[0], i1s.at[o])
    for o in range(7):
        sent(i1.at[0], i2s.at[o])

    @pl.when(home)
    def _():
        for dx in range(1, 4):
            sent(pn.at[0, 0], psend_sem.at[dx - 1])
            sent(pw.at[0, 0], psend_sem.at[dx + 2])
    for o in range(1, 8):
        sent(w_cols.at[0], w1s.at[o - 1])
        sent(wf.at[0], w2s.at[o - 1])

    shipped(osend, olast, or_sem.at[ITERS - 1])
    for e in range(2):
        for h in range(2):
            a, b = olast[4 * e + 2 * h].astype(F32), olast[4 * e + 2 * h + 1].astype(F32)
            cols = slice(128 * h, 128 * h + 128)
            ro_ref[e, 0:64, cols] = rs[e, 0:64, cols] - alpha * jnp.where(left, a, swap(b))
            ro_ref[e, 64:128, cols] = rs[e, 64:128, cols] - alpha * jnp.where(left, swap(a), b)


def hand_over(x_in, r_in, x_out, r_out, x_held, r_held, sem):
    steps = ((x_in, x_held, x_out), (r_in, r_held, r_out))
    ins = [pltpu.make_async_copy(a, held, sem.at[n]) for n, (a, held, b) in enumerate(steps)]
    outs = [pltpu.make_async_copy(held, b, sem.at[2 + n]) for n, (a, held, b) in enumerate(steps)]
    for copy in ins:
        copy.start()
    for arrived, copy in zip(ins, outs):
        arrived.wait()
        copy.start()
    for copy in outs:
        copy.wait()


def per_device(right_side, spatial_basis, temporal_basis, spectral_weight, pierce_nodes, pierce_weights):
    vm = pltpu.VMEM
    dma = pltpu.SemaphoreType.DMA
    scratch = [
        vm((2, 128, 256), F32),
        vm((1024, 1024), BF16),
        vm((4, 256, 1024), BF16),
        vm((1024, 1024), BF16),
        vm((2048, 2048), BF16),
        vm((2048, 2048), BF16),
        vm((32, 1024), F32),
        vm((2, 2, 4, 512), jnp.int32),
        vm((2, 2, 4, 512), F32),
        vm((4, 512), jnp.int32),
        vm((4, 512), F32),
        vm((512, 1024), BF16),
        vm((1024, 512), BF16),
        vm((32, 32, 32), F32),
        vm((4, 2, 64, 128), BF16),
        vm((8, 64, 128), BF16),
        vm((8, 64, 128), BF16),
        vm((8, 64, 128), F32),
        vm((8, 64, 128), F32),
        vm((8, 64, 128), F32),
        vm((8, 2, 64, 128), BF16),
        vm((32, 16, 128), BF16),
        vm((32, 16, 128), BF16),
        vm((32, 2048), BF16),
        vm((32, 2048), F32),
        vm((32, 2048), F32),
        vm((32, 2048), F32),
        vm((32, 2048), F32),
        vm((8, 32, 32), F32),
        vm((8, 32, 256), F32),
        vm((32, 2048), BF16),
        vm((32, 16, 128), BF16),
        vm((32, 16, 128), BF16),
        vm((32, 2, 16, 128), BF16),
        vm((512, 128), F32),
        vm((512, 128), F32),
        vm((512, 128), F32),
        vm((512, 128), F32),
        vm((512, 128), BF16),
        vm((1024, 128), F32),
        vm((2, 2, 16, 8, 128), F32),
        vm((4, 8, 128), F32),
        vm((2, 128, 256), F32),
        vm((2, 128, 256), F32),
        vm((2, 128, 256), F32),
        vm((8, 64, 128), BF16),
        vm((ITERS - 1, 8, 64, 128), BF16),
        vm((8, 64, 128), BF16),
        dma((6,)),
        dma((3,)),
        dma((3,)),
        dma((7,)),
        dma,
        dma((6,)),
        dma((2,)),
        dma((7,)),
        dma,
        dma((7,)),
        dma,
        dma,
        dma((4,)),
        dma,
        dma((4,)),
        dma((2, 2)),
        dma((2, 2)),
        dma((8,)),
        dma((ITERS,)),
    ]
    out = jax.ShapeDtypeStruct(right_side.shape, F32)
    results = pl.pallas_call(
        kernel,
        out_shape=(out, out),
        in_specs=[pl.BlockSpec(memory_space=pl.ANY)] * 6,
        out_specs=(pl.BlockSpec(memory_space=pltpu.VMEM),) * 2,
        scratch_shapes=scratch,
        name="cg",
        compiler_params=pltpu.CompilerParams(
            collective_id=0, has_side_effects=True, vmem_limit_bytes=56 * 2**20
        ),
    )(right_side, spatial_basis, temporal_basis, spectral_weight.T, pierce_nodes, pierce_weights)
    anywhere = (pl.BlockSpec(memory_space=pl.ANY),) * 2
    return pl.pallas_call(
        hand_over,
        out_shape=(out, out),
        in_specs=anywhere,
        out_specs=anywhere,
        scratch_shapes=[vm(right_side.shape, F32)] * 2 + [dma((4,))],
        compiler_params=pltpu.CompilerParams(vmem_limit_bytes=60 * 2**20),
        name="hand_over",
    )(*results)


def solution(mesh):
    placed = (
        P("dir", "space", "tm"),
        P(),
        P(),
        P(None, ("space", "tm")),
        P("dir", "tm", None, None),
        P("dir", "tm", None, None),
    )
    return jax.shard_map(
        per_device,
        mesh=mesh,
        in_specs=placed,
        out_specs=(P("dir", "space", "tm"), P("dir", "space", "tm")),
        check_vma=False,
    )
```

```python
import jax
import jax.numpy as jnp
from jax import lax
from jax.experimental import pallas as pl
from jax.experimental.pallas import tpu as pltpu
from jax.sharding import PartitionSpec as P

ITERS = 4
MESH = pl.DeviceIdType.MESH
F32 = jnp.float32
BF16 = jnp.bfloat16


def hops(dy, dx):
    return min(dy, 4 - dy) + min(dx, 4 - dx)


CHIPS = sorted(((dy, dx) for dy in range(4) for dx in range(4)), key=lambda o: (hops(*o), o))
RANKS = [(dy, dc, dx) for dy, dx in CHIPS for dc in range(2)]
BACK = [RANKS.index((-dy % 4, dc, -dx % 4)) for dy, dc, dx in RANKS]
FAR_Z = (4, 3, 5, 2, 6, 1, 7)
FWD_SEND, FWD_WAIT = ((24, 32), (16, 24), (8, 16), (0, 8)), ((0, 8), (8, 16), (16, 24), (24, 32))
BACK_SEND, BACK_WAIT = FWD_SEND, FWD_WAIT


def group_of(groups, rank):
    return [a <= rank < b for a, b in groups].index(True)


def dot(a, b):
    return jnp.dot(a, b, preferred_element_type=F32)


def swap(a):
    flat = a.reshape(-1, 128)
    return pltpu.roll(flat, 64, 1).reshape(a.shape)


def fold(a):
    return jnp.sum(a.reshape(-1, 8, 128), axis=0)


def total(a):
    return jnp.sum(jnp.sum(a, axis=0, keepdims=True), axis=1, keepdims=True)


def kernel(
    rs_hbm, s_hbm, t_hbm, w_hbm, pn_hbm, pw_hbm,
    xo_ref, ro_ref,
    rs, sn, s4, st, tb, tt, w_in, pn, pw, pnode, pwgt, g, gt,
    w_cols, isend, i1, i2, im, r, q, vb, fsend, frecv, ua, xv_, xm, xq, xd, wslot, wf, zb, bsend, brecv, vk,
    pr, pq, pd, pv_, pb, yacc, red, scal, xb, db, qb, osend, orecv, olast,
    load_sem, i1s, i1r, i2s, i2r, psend_sem, precv_sem, w1s, w1r, w2s, w2r,
    fs_sem, fr_sem, bs_sem, br_sem, rs_sem, rr_sem, os_sem, or_sem,
):
    z = lax.axis_index("space")
    m = lax.axis_index("tm")
    x = lax.axis_index("dir")
    y, core = m // 2, m % 2
    p = m * 4 + x
    left = lax.broadcasted_iota(jnp.int32, (1, 128), 1) < 64
    home = z // 2 == x

    def dev(zz, mm, xx):
        return {"space": zz, "tm": mm, "dir": xx}

    def remote(src, dst, ss, rsem, to):
        return pltpu.make_async_remote_copy(
            src_ref=src, dst_ref=dst, send_sem=ss, recv_sem=rsem, device_id=to, device_id_type=MESH
        )

    def peer(j):
        dy, dc, dx = RANKS[j]
        return 2 * ((y + dy) % 4) + (core + dc) % 2, (x + dx) % 4

    barrier = pltpu.get_barrier_semaphore()

    def greet(to):
        pl.semaphore_signal(barrier, inc=1, device_id=to, device_id_type=MESH)

    for o in FAR_Z:
        for dc in range(2):
            greet(dev((z + o) % 8, 2 * y + (core + dc) % 2, x))
    for j in reversed(range(1, 32)):
        greet(dev(z, *peer(j)))

    loads = [
        pltpu.make_async_copy(rs_hbm, rs, load_sem.at[0]),
        pltpu.make_async_copy(pn_hbm, pn, load_sem.at[1]),
        pltpu.make_async_copy(pw_hbm, pw, load_sem.at[2]),
        pltpu.make_async_copy(w_hbm, w_in, load_sem.at[3]),
    ]
    s_load = pltpu.make_async_copy(s_hbm, sn, load_sem.at[4])

    def block(j):
        mm, xx = peer(j)
        return mm * 4 + xx

    for copy in loads + [s_load]:
        copy.start()
    for j in range(32):
        rows = pl.ds(pl.multiple_of(block(j) * 64, 64), 64)
        pltpu.make_async_copy(t_hbm.at[rows], tb.at[pl.ds(64 * j, 64)], load_sem.at[5]).start()

    loads[0].wait()
    for h in range(2):
        for e in range(2):
            c = rs[e, :, 128 * h:128 * h + 128]
            top, bottom = c[:64], c[64:]
            isend[2 * h, e] = jnp.where(left, top, swap(bottom)).astype(BF16)
            isend[2 * h + 1, e] = jnp.where(left, swap(top), bottom).astype(BF16)
    i1[pl.ds(2 * x, 2)] = isend[x]
    for copy in loads[1:]:
        copy.wait()
    w_cols[...] = w_in[...].T.reshape(32, 32, 32).astype(BF16)

    pl.semaphore_wait(barrier, 45)

    for dx in (2, 1, 3):
        xx = (x + dx) % 4
        remote(isend.at[xx], i1.at[pl.ds(2 * x, 2)], i1s.at[dx - 1], i1r.at[dx - 1], dev(z, m, xx)).start()
    e_here = z % 2

    @pl.when(home)
    def _():
        for dx in range(1, 4):
            xx = (x + dx) % 4
            remote(pn.at[e_here, xx // 2], pnode, psend_sem.at[dx - 1], precv_sem.at[0], dev(z, m, xx)).start()
            remote(pw.at[e_here, xx // 2], pwgt, psend_sem.at[dx + 2], precv_sem.at[1], dev(z, m, xx)).start()
        pltpu.make_async_copy(pn.at[e_here, x // 2], pnode, precv_sem.at[0]).start()
        pltpu.make_async_copy(pw.at[e_here, x // 2], pwgt, precv_sem.at[1]).start()
    for o in range(1, 8):
        mm = (m + o) % 8
        remote(w_cols.at[mm * 4 + x], wslot.at[m], w1s.at[o - 1], w1r, dev(z, mm, x)).start()
    pltpu.make_async_copy(w_cols.at[p], wslot.at[m], w1r).start()

    def forward(xx):
        for e in range(2):
            zz = 2 * xx + e

            @pl.when(zz != z)
            def _():
                remote(i1.at[zz], i2.at[z], i2s.at[(zz + 7 - z) % 8], i2r, dev(zz, m, x)).start()

            @pl.when(zz == z)
            def _():
                pltpu.make_async_copy(i1.at[zz], i2.at[z], i2r).start()

    forward(x)
    s_load.wait()
    s4[...] = sn[...].T.reshape(4, 256, 1024)
    for j in range(32):
        own = block(j)
        st[32 * j:32 * j + 32, :] = s4[own // 8, pl.ds(pl.multiple_of(own % 8 * 32, 32), 32), :]
    for c in range(4):
        sn[:, 256 * c:256 * c + 256] = st[256 * c:256 * c + 256, :].T
    for dx in (1, 3, 2):
        xx = (x + 4 - dx) % 4
        span = i1.at[pl.ds(2 * xx, 2)]
        remote(span, span, i1s.at[dx - 1], i1r.at[dx - 1], dev(z, m, x)).wait_recv()
        forward(xx)

    pltpu.make_async_copy(wslot, wslot, w1r).wait()
    own_w = wf.at[z]
    for h in range(2):
        own_w[:, 128 * h:128 * h + 128] = jnp.concatenate([wslot[4 * h + i].astype(F32) for i in range(4)], axis=1).astype(BF16)

    for ref in (r, q, xm, xq, xd, pr, pq, pd, xb, db, qb):
        ref[...] = jnp.zeros_like(ref)
    scal[0:2] = jnp.ones((2, 8, 128), F32)
    scal[2] = jnp.full((8, 128), -1.0, F32)
    scal[3] = jnp.zeros((8, 128), F32)

    pltpu.make_async_copy(pnode, pnode, precv_sem.at[0]).wait()
    pltpu.make_async_copy(pwgt, pwgt, precv_sem.at[1]).wait()
    nodes, wgts = pnode[...], pwgt[...]
    nodes_t = jnp.concatenate([nodes, nodes], axis=0).astype(F32).T.astype(jnp.int32)
    wgts_t = jnp.concatenate([wgts, wgts], axis=0).T
    for c in range(8):
        ids = lax.broadcasted_iota(jnp.int32, (128, 512), 0) + 128 * c
        acc = jnp.zeros((128, 512), F32)
        for j in range(4):
            acc += jnp.where(nodes[j:j + 1] == ids, wgts[j:j + 1], 0.0)
        gt[128 * c:128 * c + 128, :] = acc.astype(BF16)
        ids = lax.broadcasted_iota(jnp.int32, (512, 128), 1) + 128 * c
        acc = jnp.zeros((512, 128), F32)
        for j in range(4):
            acc += jnp.where(nodes_t[:, j:j + 1] == ids, wgts_t[:, j:j + 1], 0.0)
        g[:, 128 * c:128 * c + 128] = acc.astype(BF16)

    def transpose(c):
        @pl.loop(0, 8)
        def _(i):
            cols = pl.ds(pl.multiple_of(i * 256, 256), 256)
            tt[cols, 512 * c:512 * c + 512] = tb[512 * c:512 * c + 512, cols].T

    pltpu.make_async_copy(t_hbm, tb, load_sem.at[5]).wait()
    for c in range(2, 4):
        transpose(c)

    pltpu.make_async_copy(i2, i2, i2r).wait()
    for o in FAR_Z:
        remote(wf.at[z], wf.at[z], w2s.at[o - 1], w2r, dev((z + o) % 8, m, x)).start()
    first = i2[...].astype(F32)
    turned = swap(first)
    im[...] = first
    vb[:, 0] = jnp.where(left, first, turned).astype(BF16)
    vb[:, 1] = jnp.where(left, turned, first).astype(BF16)

    def reduce_start(par, step, value):
        own = (y * 4 + x, z * 2 + core)[step]
        slot = red.at[par, step, own]
        slot[...] = value
        if step == 0:
            where = [dev(z, 2 * ((y + dy) % 4) + core, (x + dx) % 4) for dy, dx in reversed(CHIPS[1:])]
        else:
            where = [dev((z + o) % 8, 2 * y + (core + dc) % 2, x) for o in FAR_Z for dc in range(2)]
            where.append(dev(z, 2 * y + 1 - core, x))
        for to in where:
            remote(slot, slot, rs_sem.at[par, step], rr_sem.at[par, step], to).start()

    def reduce_finish(par, step):
        span = red.at[par, step, pl.ds(0, 15)]
        both = remote(span, span, rs_sem.at[par, step], rr_sem.at[par, step], dev(z, m, x))
        both.wait_recv()
        both.wait_send()
        return jnp.sum(red[par, step], axis=0)

    def send_group(ranks, groups, src, dst, ssem, rsem):
        for j in reversed(range(*ranks)):
            if j > 0:
                sem = rsem.at[group_of(groups, BACK[j])]
                remote(src.at[j], dst.at[BACK[j]], ssem, sem, dev(z, *peer(j))).start()

    def wait_group(ranks, groups, buf, rsem):
        a, b = ranks
        span = buf.at[pl.ds(0, b - max(a, 1))]
        sem = rsem.at[groups.index(ranks)]
        remote(span, span, sem, sem, dev(z, m, x)).wait_recv()

    def wait_sent(buf, ssem):
        span = buf.at[pl.ds(0, 31)]
        remote(span, span, ssem, ssem, dev(z, m, x)).wait_send()

    def scalars(j):
        sums = jnp.sum(reduce_finish(j % 2, 1), axis=1, keepdims=True)
        rr, ra, rb = sums[0:1], sums[1:2], sums[2:3]
        beta = jnp.where(j == 0, 0.0, rr / scal[0, 0:1, 0:1])
        curve = ra + beta * (2.0 * rb + beta * scal[1, 0:1, 0:1])
        for n, value in enumerate((rr, curve, rr / curve, beta)):
            scal[n] = jnp.broadcast_to(value, (8, 128))

    def factors():
        return scal[2, 0:1, 0:1], scal[3, 0:1, 0:1]

    slot_out = (z % 2) * 4 + x

    def ship(src, dst, sem):
        for o in FAR_Z + (0,):
            zz = (z + o) % 8

            def send():
                remote(src.at[zz], dst.at[slot_out], os_sem.at[o], sem, dev(zz, m, z // 2)).start()
            if o == 0:
                pl.when(jnp.logical_not(home))(send)

                @pl.when(home)
                def _():
                    pltpu.make_async_copy(src.at[zz], dst.at[slot_out], sem).start()
            else:
                send()

    def shipped(src, dst, sem):
        pltpu.make_async_copy(dst, dst, sem).wait()
        for o in range(8):
            if o == 0:
                @pl.when(jnp.logical_not(home))
                def _():
                    sent(src.at[0], os_sem.at[o])
            else:
                sent(src.at[0], os_sem.at[o])

    def sent(src, sem):
        remote(src, src, sem, sem, dev(z, m, x)).wait_send()

    def advance(tiles):
        alpha, beta = factors()
        for e in range(2):
            for h in range(2):
                a, b = tiles[4 * e + 2 * h].astype(F32), tiles[4 * e + 2 * h + 1].astype(F32)
                for part, rows in ((jnp.where(left, a, swap(b)), slice(0, 64)), (jnp.where(left, swap(a), b), slice(64, 128))):
                    at = (e, rows, slice(128 * h, 128 * h + 128))
                    qn = part + beta * qb[at]
                    dn = rs[at] + beta * db[at]
                    qb[at] = qn
                    db[at] = dn
                    xb[at] += alpha * dn
                    rs[at] -= alpha * qn

    @pl.loop(0, ITERS)
    def _(it):
        par = it % 2
        vbv = vb[...].reshape(1024, 128)
        for a, b in FWD_SEND:
            u = dot(st[32 * a:32 * b, :], vbv).reshape(b - a, 2, 16, 128)
            fsend[a:b] = jnp.where(left, u[:, 0], u[:, 1]).astype(BF16)
            send_group((a, b), FWD_WAIT, fsend, frecv, fs_sem, fr_sem)
        frecv[0] = fsend[0]

        @pl.when(it == 0)
        def _():
            for c in range(2):
                transpose(c)

        @pl.when(it > 0)
        def _():
            osend[...] = im[...].astype(BF16)
            ship(osend, orecv.at[it - 1], or_sem.at[it - 1])

        pv_[...] = dot(g[...], vbv)
        v = im[...].reshape(512, 128)

        def modes(ranks):
            a, b = ranks
            wait_group(ranks, FWD_WAIT, frecv, fr_sem)
            tiles = frecv[a:b].astype(F32)
            swapped = swap(tiles)
            for j in range((b - a) // 2):
                ua[0:16, 128 * j:128 * j + 128] = jnp.where(left, tiles[2 * j], swapped[2 * j + 1]).astype(BF16)
                ua[16:32, 128 * j:128 * j + 128] = jnp.where(left, swapped[2 * j], tiles[2 * j + 1]).astype(BF16)
            xv = dot(ua[:, :64 * (b - a)], tb[64 * a:64 * b, :])
            if ranks == FWD_WAIT[0]:
                xv_[...] = xv
            else:
                xv_[...] += xv

        @pl.when(it > 0)
        def _():
            scalars(it - 1)

        alpha, beta = factors()
        pold = pr[...] + beta * pd[...]
        pd[...] = pold
        pqn = pv_[...] + beta * pq[...]
        pq[...] = pqn
        pnew = pr[...] - alpha * pqn
        pr[...] = pnew
        pb[...] = pnew.astype(BF16)
        qn = v + beta * q[...].reshape(512, 128)
        q[...] = qn.reshape(8, 64, 128)
        rn = r[...].reshape(512, 128) - alpha * qn
        r[...] = rn.reshape(8, 64, 128)
        norm = fold(rn * rn)
        suma = 0.5 * fold(pnew * pnew)
        sumb = 0.5 * fold(pnew * pold)
        xd[...] = xm[...] + beta * xd[...]
        for ranks in FWD_WAIT:
            modes(ranks)
        wait_sent(fsend, fs_sem)

        @pl.when(it == 0)
        def _():
            pltpu.make_async_copy(wf.at[pl.ds(0, 7)], wf.at[pl.ds(0, 7)], w2r).wait()

        for zz in range(8):
            cols = slice(256 * zz, 256 * zz + 256)
            xqn = xv_[:, cols] + beta * xq[:, cols]
            xq[:, cols] = xqn
            xn = xm[:, cols] - alpha * xqn
            xm[:, cols] = xn
            wx = wf[zz].astype(F32) * xn
            zb[:, cols] = wx.astype(BF16)
            qa, qc = wx * xn, wx * xd[:, cols]
            suma += fold(qa[:, :128] + qa[:, 128:])
            sumb += fold(qc[:, :128] + qc[:, 128:])
        row = lax.broadcasted_iota(jnp.int32, (8, 128), 0)
        one = [jnp.sum(part, axis=0, keepdims=True) for part in (norm, suma, sumb)]
        reduce_start(par, 0, jnp.where(row == 0, one[0], jnp.where(row == 1, one[1], one[2])))
        zv = zb[...]
        for a, b in BACK_SEND:
            w = dot(zv, tt[:, 64 * a:64 * b])
            for j in range((b - a) // 2):
                top, bottom = w[:16, 128 * j:128 * j + 128], w[16:, 128 * j:128 * j + 128]
                bsend[a + 2 * j] = jnp.where(left, top, swap(bottom)).astype(BF16)
                bsend[a + 2 * j + 1] = jnp.where(left, swap(top), bottom).astype(BF16)
            send_group((a, b), BACK_WAIT, bsend, brecv, bs_sem, br_sem)
        brecv[0] = bsend[0]
        yacc[...] = dot(gt[...], pb[...])

        @pl.when(it > 0)
        def _():
            shipped(osend, orecv.at[it - 1], or_sem.at[it - 1])
            advance(orecv.at[it - 1])

        part = reduce_finish(par, 0)
        reduce_start(par, 1, part)
        for ranks in BACK_WAIT:
            a, b = ranks
            wait_group(ranks, BACK_WAIT, brecv, br_sem)
            tiles = brecv[a:b].astype(F32)
            swapped = swap(tiles)
            vk[a:b, 0] = jnp.where(left, tiles, swapped).astype(BF16)
            vk[a:b, 1] = jnp.where(left, swapped, tiles).astype(BF16)
            part = yacc[...] + dot(sn[:, 32 * a:32 * b], vk[a:b].reshape(32 * (b - a), 128))
            if ranks != BACK_WAIT[-1]:
                yacc[...] = part
        wait_sent(bsend, bs_sem)
        ya = part.reshape(8, 2, 64, 128)
        vb[...] = ya.astype(BF16)
        im[...] = jnp.where(left, ya[:, 0], ya[:, 1])

    osend[...] = im[...].astype(BF16)
    ship(osend, olast, or_sem.at[ITERS - 1])
    scalars(ITERS - 1)
    alpha, beta = factors()
    xo_ref[...] = xb[...] + alpha * (rs[...] + beta * db[...])
    rs[...] = rs[...] - (alpha * beta) * qb[...]

    for o in range(3):
        sent(isend.at[0], i1s.at[o])
    for o in range(7):
        sent(i1.at[0], i2s.at[o])

    @pl.when(home)
    def _():
        for dx in range(1, 4):
            sent(pn.at[0, 0], psend_sem.at[dx - 1])
            sent(pw.at[0, 0], psend_sem.at[dx + 2])
    for o in range(1, 8):
        sent(w_cols.at[0], w1s.at[o - 1])
        sent(wf.at[0], w2s.at[o - 1])

    shipped(osend, olast, or_sem.at[ITERS - 1])
    for e in range(2):
        for h in range(2):
            a, b = olast[4 * e + 2 * h].astype(F32), olast[4 * e + 2 * h + 1].astype(F32)
            cols = slice(128 * h, 128 * h + 128)
            ro_ref[e, 0:64, cols] = rs[e, 0:64, cols] - alpha * jnp.where(left, a, swap(b))
            ro_ref[e, 64:128, cols] = rs[e, 64:128, cols] - alpha * jnp.where(left, swap(a), b)


def hand_over(x_in, r_in, x_out, r_out, x_held, r_held, sem):
    steps = ((x_in, x_held, x_out), (r_in, r_held, r_out))
    ins = [pltpu.make_async_copy(a, held, sem.at[n]) for n, (a, held, b) in enumerate(steps)]
    outs = [pltpu.make_async_copy(held, b, sem.at[2 + n]) for n, (a, held, b) in enumerate(steps)]
    for copy in ins:
        copy.start()
    for arrived, copy in zip(ins, outs):
        arrived.wait()
        copy.start()
    for copy in outs:
        copy.wait()


def per_device(right_side, spatial_basis, temporal_basis, spectral_weight, pierce_nodes, pierce_weights):
    vm = pltpu.VMEM
    dma = pltpu.SemaphoreType.DMA
    scratch = [
        vm((2, 128, 256), F32),
        vm((1024, 1024), BF16),
        vm((4, 256, 1024), BF16),
        vm((1024, 1024), BF16),
        vm((2048, 2048), BF16),
        vm((2048, 2048), BF16),
        vm((32, 1024), F32),
        vm((2, 2, 4, 512), jnp.int32),
        vm((2, 2, 4, 512), F32),
        vm((4, 512), jnp.int32),
        vm((4, 512), F32),
        vm((512, 1024), BF16),
        vm((1024, 512), BF16),
        vm((32, 32, 32), BF16),
        vm((4, 2, 64, 128), BF16),
        vm((8, 64, 128), BF16),
        vm((8, 64, 128), BF16),
        vm((8, 64, 128), F32),
        vm((8, 64, 128), F32),
        vm((8, 64, 128), F32),
        vm((8, 2, 64, 128), BF16),
        vm((32, 16, 128), BF16),
        vm((32, 16, 128), BF16),
        vm((32, 2048), BF16),
        vm((32, 2048), F32),
        vm((32, 2048), F32),
        vm((32, 2048), F32),
        vm((32, 2048), F32),
        vm((8, 32, 32), BF16),
        vm((8, 32, 256), BF16),
        vm((32, 2048), BF16),
        vm((32, 16, 128), BF16),
        vm((32, 16, 128), BF16),
        vm((32, 2, 16, 128), BF16),
        vm((512, 128), F32),
        vm((512, 128), F32),
        vm((512, 128), F32),
        vm((512, 128), F32),
        vm((512, 128), BF16),
        vm((1024, 128), F32),
        vm((2, 2, 16, 8, 128), F32),
        vm((4, 8, 128), F32),
        vm((2, 128, 256), F32),
        vm((2, 128, 256), F32),
        vm((2, 128, 256), F32),
        vm((8, 64, 128), BF16),
        vm((ITERS - 1, 8, 64, 128), BF16),
        vm((8, 64, 128), BF16),
        dma((6,)),
        dma((3,)),
        dma((3,)),
        dma((7,)),
        dma,
        dma((6,)),
        dma((2,)),
        dma((7,)),
        dma,
        dma((7,)),
        dma,
        dma,
        dma((4,)),
        dma,
        dma((4,)),
        dma((2, 2)),
        dma((2, 2)),
        dma((8,)),
        dma((ITERS,)),
    ]
    out = jax.ShapeDtypeStruct(right_side.shape, F32)
    results = pl.pallas_call(
        kernel,
        out_shape=(out, out),
        in_specs=[pl.BlockSpec(memory_space=pl.ANY)] * 6,
        out_specs=(pl.BlockSpec(memory_space=pltpu.VMEM),) * 2,
        scratch_shapes=scratch,
        name="cg",
        compiler_params=pltpu.CompilerParams(
            collective_id=0, has_side_effects=True, vmem_limit_bytes=56 * 2**20
        ),
    )(right_side, spatial_basis, temporal_basis, spectral_weight.T, pierce_nodes, pierce_weights)
    anywhere = (pl.BlockSpec(memory_space=pl.ANY),) * 2
    return pl.pallas_call(
        hand_over,
        out_shape=(out, out),
        in_specs=anywhere,
        out_specs=anywhere,
        scratch_shapes=[vm(right_side.shape, F32)] * 2 + [dma((4,))],
        compiler_params=pltpu.CompilerParams(vmem_limit_bytes=60 * 2**20),
        name="hand_over",
    )(*results)


def solution(mesh):
    placed = (
        P("dir", "space", "tm"),
        P(),
        P(),
        P(None, ("space", "tm")),
        P("dir", "tm", None, None),
        P("dir", "tm", None, None),
    )
    return jax.shard_map(
        per_device,
        mesh=mesh,
        in_specs=placed,
        out_specs=(P("dir", "space", "tm"), P("dir", "space", "tm")),
        check_vma=False,
    )
```

```python
import jax
import jax.numpy as jnp
from jax import lax
from jax.experimental import pallas as pl
from jax.experimental.pallas import tpu as pltpu
from jax.sharding import PartitionSpec as P

ITERS = 4
MESH = pl.DeviceIdType.MESH
F32 = jnp.float32
BF16 = jnp.bfloat16


def hops(dy, dx):
    return min(dy, 4 - dy) + min(dx, 4 - dx)


CHIPS = sorted(((dy, dx) for dy in range(4) for dx in range(4)), key=lambda o: (hops(*o), o))
RANKS = [(dy, dc, dx) for dy, dx in CHIPS for dc in range(2)]
BACK = [RANKS.index((-dy % 4, dc, -dx % 4)) for dy, dc, dx in RANKS]
FAR_Z = (4, 3, 5, 2, 6, 1, 7)
FWD_SEND, FWD_WAIT = ((24, 32), (16, 24), (8, 16), (0, 8)), ((0, 8), (8, 16), (16, 24), (24, 32))
BACK_SEND, BACK_WAIT = FWD_SEND, FWD_WAIT


def group_of(groups, rank):
    return [a <= rank < b for a, b in groups].index(True)


def dot(a, b):
    return jnp.dot(a, b, preferred_element_type=F32)


def swap(a):
    flat = a.reshape(-1, 128)
    return pltpu.roll(flat, 64, 1).reshape(a.shape)


def fold(a):
    return jnp.sum(a.reshape(-1, 8, 128), axis=0)


def total(a):
    return jnp.sum(jnp.sum(a, axis=0, keepdims=True), axis=1, keepdims=True)


def kernel(
    rs_hbm, s_hbm, t_hbm, w_hbm, pn_hbm, pw_hbm,
    xo_ref, ro_ref,
    rs, sn, s4, st, tb, tt, w_in, pn, pw, pnode, pwgt, g, gt,
    w_cols, isend, i1, i2, im, r, q, vb, fsend, frecv, ua, xv_, xm, xq, xd, wslot, wf, zb, bsend, brecv, vk,
    pr, pq, pd, pv_, pb, yacc, red, scal, xb, db, qb, osend, orecv, olast,
    load_sem, i1s, i1r, i2s, i2r, psend_sem, precv_sem, w1s, w1r, w2s, w2r,
    fs_sem, fr_sem, bs_sem, br_sem, rs_sem, rr_sem, os_sem, or_sem,
):
    z = lax.axis_index("space")
    m = lax.axis_index("tm")
    x = lax.axis_index("dir")
    y, core = m // 2, m % 2
    p = m * 4 + x
    left = lax.broadcasted_iota(jnp.int32, (1, 128), 1) < 64
    home = z // 2 == x

    def dev(zz, mm, xx):
        return {"space": zz, "tm": mm, "dir": xx}

    def remote(src, dst, ss, rsem, to):
        return pltpu.make_async_remote_copy(
            src_ref=src, dst_ref=dst, send_sem=ss, recv_sem=rsem, device_id=to, device_id_type=MESH
        )

    def peer(j):
        dy, dc, dx = RANKS[j]
        return 2 * ((y + dy) % 4) + (core + dc) % 2, (x + dx) % 4

    barrier = pltpu.get_barrier_semaphore()

    def greet(to):
        pl.semaphore_signal(barrier, inc=1, device_id=to, device_id_type=MESH)

    for o in FAR_Z:
        greet(dev((z + o) % 8, m, x))
    for o in range(1, 8):
        greet(dev(z, (m + o) % 8, x))
    for o in (2, 1, 3):
        greet(dev(z, m, (x + o) % 4))

    loads = [
        pltpu.make_async_copy(rs_hbm, rs, load_sem.at[0]),
        pltpu.make_async_copy(pn_hbm, pn, load_sem.at[1]),
        pltpu.make_async_copy(pw_hbm, pw, load_sem.at[2]),
        pltpu.make_async_copy(w_hbm, w_in, load_sem.at[3]),
    ]
    s_load = pltpu.make_async_copy(s_hbm, sn, load_sem.at[4])

    def block(j):
        mm, xx = peer(j)
        return mm * 4 + xx

    for copy in loads + [s_load]:
        copy.start()
    for j in range(32):
        rows = pl.ds(pl.multiple_of(block(j) * 64, 64), 64)
        pltpu.make_async_copy(t_hbm.at[rows], tb.at[pl.ds(64 * j, 64)], load_sem.at[5]).start()

    loads[0].wait()
    for h in range(2):
        for e in range(2):
            c = rs[e, :, 128 * h:128 * h + 128]
            top, bottom = c[:64], c[64:]
            isend[2 * h, e] = jnp.where(left, top, swap(bottom)).astype(BF16)
            isend[2 * h + 1, e] = jnp.where(left, swap(top), bottom).astype(BF16)
    i1[pl.ds(2 * x, 2)] = isend[x]
    for copy in loads[1:]:
        copy.wait()
    w_cols[...] = w_in[...].T.reshape(32, 32, 32).astype(BF16)

    pl.semaphore_wait(barrier, 17)

    for dx in (2, 1, 3):
        xx = (x + dx) % 4
        remote(isend.at[xx], i1.at[pl.ds(2 * x, 2)], i1s.at[dx - 1], i1r.at[dx - 1], dev(z, m, xx)).start()
    e_here = z % 2

    @pl.when(home)
    def _():
        for dx in range(1, 4):
            xx = (x + dx) % 4
            remote(pn.at[e_here, xx // 2], pnode, psend_sem.at[dx - 1], precv_sem.at[0], dev(z, m, xx)).start()
            remote(pw.at[e_here, xx // 2], pwgt, psend_sem.at[dx + 2], precv_sem.at[1], dev(z, m, xx)).start()
        pltpu.make_async_copy(pn.at[e_here, x // 2], pnode, precv_sem.at[0]).start()
        pltpu.make_async_copy(pw.at[e_here, x // 2], pwgt, precv_sem.at[1]).start()
    for o in range(1, 8):
        mm = (m + o) % 8
        remote(w_cols.at[mm * 4 + x], wslot.at[m], w1s.at[o - 1], w1r, dev(z, mm, x)).start()
    pltpu.make_async_copy(w_cols.at[p], wslot.at[m], w1r).start()

    def forward(xx):
        for e in range(2):
            zz = 2 * xx + e

            @pl.when(zz != z)
            def _():
                remote(i1.at[zz], i2.at[z], i2s.at[(zz + 7 - z) % 8], i2r, dev(zz, m, x)).start()

            @pl.when(zz == z)
            def _():
                pltpu.make_async_copy(i1.at[zz], i2.at[z], i2r).start()

    forward(x)
    s_load.wait()
    s4[...] = sn[...].T.reshape(4, 256, 1024)
    for j in range(32):
        own = block(j)
        st[32 * j:32 * j + 32, :] = s4[own // 8, pl.ds(pl.multiple_of(own % 8 * 32, 32), 32), :]
    for c in range(4):
        sn[:, 256 * c:256 * c + 256] = st[256 * c:256 * c + 256, :].T
    for dx in (1, 3, 2):
        xx = (x + 4 - dx) % 4
        span = i1.at[pl.ds(2 * xx, 2)]
        remote(span, span, i1s.at[dx - 1], i1r.at[dx - 1], dev(z, m, x)).wait_recv()
        forward(xx)

    pltpu.make_async_copy(wslot, wslot, w1r).wait()
    own_w = wf.at[z]
    for h in range(2):
        own_w[:, 128 * h:128 * h + 128] = jnp.concatenate([wslot[4 * h + i].astype(F32) for i in range(4)], axis=1).astype(BF16)

    for ref in (r, q, xm, xq, xd, pr, pq, pd, xb, db, qb):
        ref[...] = jnp.zeros_like(ref)
    scal[0:2] = jnp.ones((2, 8, 128), F32)
    scal[2] = jnp.full((8, 128), -1.0, F32)
    scal[3] = jnp.zeros((8, 128), F32)

    pltpu.make_async_copy(pnode, pnode, precv_sem.at[0]).wait()
    pltpu.make_async_copy(pwgt, pwgt, precv_sem.at[1]).wait()
    nodes, wgts = pnode[...], pwgt[...]
    nodes_t = jnp.concatenate([nodes, nodes], axis=0).astype(F32).T.astype(jnp.int32)
    wgts_t = jnp.concatenate([wgts, wgts], axis=0).T
    for c in range(8):
        ids = lax.broadcasted_iota(jnp.int32, (128, 512), 0) + 128 * c
        acc = jnp.zeros((128, 512), F32)
        for j in range(4):
            acc += jnp.where(nodes[j:j + 1] == ids, wgts[j:j + 1], 0.0)
        gt[128 * c:128 * c + 128, :] = acc.astype(BF16)
        ids = lax.broadcasted_iota(jnp.int32, (512, 128), 1) + 128 * c
        acc = jnp.zeros((512, 128), F32)
        for j in range(4):
            acc += jnp.where(nodes_t[:, j:j + 1] == ids, wgts_t[:, j:j + 1], 0.0)
        g[:, 128 * c:128 * c + 128] = acc.astype(BF16)

    def transpose(c):
        @pl.loop(0, 8)
        def _(i):
            cols = pl.ds(pl.multiple_of(i * 256, 256), 256)
            tt[cols, 512 * c:512 * c + 512] = tb[512 * c:512 * c + 512, cols].T

    pltpu.make_async_copy(t_hbm, tb, load_sem.at[5]).wait()
    for c in range(2, 4):
        transpose(c)

    pltpu.make_async_copy(i2, i2, i2r).wait()
    for o in FAR_Z:
        remote(wf.at[z], wf.at[z], w2s.at[o - 1], w2r, dev((z + o) % 8, m, x)).start()
    first = i2[...].astype(F32)
    turned = swap(first)
    im[...] = first
    vb[:, 0] = jnp.where(left, first, turned).astype(BF16)
    vb[:, 1] = jnp.where(left, turned, first).astype(BF16)

    def reduce_start(par, step, value):
        own = (y * 4 + x, z * 2 + core)[step]
        slot = red.at[par, step, own]
        slot[...] = value
        if step == 0:
            where = [dev(z, 2 * ((y + dy) % 4) + core, (x + dx) % 4) for dy, dx in reversed(CHIPS[1:])]
        else:
            where = [dev((z + o) % 8, 2 * y + (core + dc) % 2, x) for o in FAR_Z for dc in range(2)]
            where.append(dev(z, 2 * y + 1 - core, x))
        for to in where:
            remote(slot, slot, rs_sem.at[par, step], rr_sem.at[par, step], to).start()

    def reduce_finish(par, step):
        span = red.at[par, step, pl.ds(0, 15)]
        both = remote(span, span, rs_sem.at[par, step], rr_sem.at[par, step], dev(z, m, x))
        both.wait_recv()
        both.wait_send()
        return jnp.sum(red[par, step], axis=0)

    def send_group(ranks, groups, src, dst, ssem, rsem):
        for j in reversed(range(*ranks)):
            if j > 0:
                sem = rsem.at[group_of(groups, BACK[j])]
                remote(src.at[j], dst.at[BACK[j]], ssem, sem, dev(z, *peer(j))).start()

    def wait_group(ranks, groups, buf, rsem):
        a, b = ranks
        span = buf.at[pl.ds(0, b - max(a, 1))]
        sem = rsem.at[groups.index(ranks)]
        remote(span, span, sem, sem, dev(z, m, x)).wait_recv()

    def wait_sent(buf, ssem):
        span = buf.at[pl.ds(0, 31)]
        remote(span, span, ssem, ssem, dev(z, m, x)).wait_send()

    def scalars(j):
        sums = jnp.sum(reduce_finish(j % 2, 1), axis=1, keepdims=True)
        rr, ra, rb = sums[0:1], sums[1:2], sums[2:3]
        beta = jnp.where(j == 0, 0.0, rr / scal[0, 0:1, 0:1])
        curve = ra + beta * (2.0 * rb + beta * scal[1, 0:1, 0:1])
        for n, value in enumerate((rr, curve, rr / curve, beta)):
            scal[n] = jnp.broadcast_to(value, (8, 128))

    def factors():
        return scal[2, 0:1, 0:1], scal[3, 0:1, 0:1]

    slot_out = (z % 2) * 4 + x

    def ship(src, dst, sem):
        for o in FAR_Z + (0,):
            zz = (z + o) % 8

            def send():
                remote(src.at[zz], dst.at[slot_out], os_sem.at[o], sem, dev(zz, m, z // 2)).start()
            if o == 0:
                pl.when(jnp.logical_not(home))(send)

                @pl.when(home)
                def _():
                    pltpu.make_async_copy(src.at[zz], dst.at[slot_out], sem).start()
            else:
                send()

    def shipped(src, dst, sem):
        pltpu.make_async_copy(dst, dst, sem).wait()
        for o in range(8):
            if o == 0:
                @pl.when(jnp.logical_not(home))
                def _():
                    sent(src.at[0], os_sem.at[o])
            else:
                sent(src.at[0], os_sem.at[o])

    def sent(src, sem):
        remote(src, src, sem, sem, dev(z, m, x)).wait_send()

    def advance(tiles):
        alpha, beta = factors()
        for e in range(2):
            for h in range(2):
                a, b = tiles[4 * e + 2 * h].astype(F32), tiles[4 * e + 2 * h + 1].astype(F32)
                for part, rows in ((jnp.where(left, a, swap(b)), slice(0, 64)), (jnp.where(left, swap(a), b), slice(64, 128))):
                    at = (e, rows, slice(128 * h, 128 * h + 128))
                    qn = part + beta * qb[at]
                    dn = rs[at] + beta * db[at]
                    qb[at] = qn
                    db[at] = dn
                    xb[at] += alpha * dn
                    rs[at] -= alpha * qn

    @pl.loop(0, ITERS)
    def _(it):
        par = it % 2
        vbv = vb[...].reshape(1024, 128)
        for a, b in FWD_SEND:
            u = dot(st[32 * a:32 * b, :], vbv).reshape(b - a, 2, 16, 128)
            fsend[a:b] = jnp.where(left, u[:, 0], u[:, 1]).astype(BF16)
            send_group((a, b), FWD_WAIT, fsend, frecv, fs_sem, fr_sem)
        frecv[0] = fsend[0]

        @pl.when(it == 0)
        def _():
            for c in range(2):
                transpose(c)

        @pl.when(it > 0)
        def _():
            osend[...] = im[...].astype(BF16)
            ship(osend, orecv.at[it - 1], or_sem.at[it - 1])

        pv_[...] = dot(g[...], vbv)
        v = im[...].reshape(512, 128)

        def modes(ranks):
            a, b = ranks
            wait_group(ranks, FWD_WAIT, frecv, fr_sem)
            tiles = frecv[a:b].astype(F32)
            swapped = swap(tiles)
            for j in range((b - a) // 2):
                ua[0:16, 128 * j:128 * j + 128] = jnp.where(left, tiles[2 * j], swapped[2 * j + 1]).astype(BF16)
                ua[16:32, 128 * j:128 * j + 128] = jnp.where(left, swapped[2 * j], tiles[2 * j + 1]).astype(BF16)
            xv = dot(ua[:, :64 * (b - a)], tb[64 * a:64 * b, :])
            if ranks == FWD_WAIT[0]:
                xv_[...] = xv
            else:
                xv_[...] += xv

        @pl.when(it > 0)
        def _():
            scalars(it - 1)

        alpha, beta = factors()
        pold = pr[...] + beta * pd[...]
        pd[...] = pold
        pqn = pv_[...] + beta * pq[...]
        pq[...] = pqn
        pnew = pr[...] - alpha * pqn
        pr[...] = pnew
        pb[...] = pnew.astype(BF16)
        qn = v + beta * q[...].reshape(512, 128)
        q[...] = qn.reshape(8, 64, 128)
        rn = r[...].reshape(512, 128) - alpha * qn
        r[...] = rn.reshape(8, 64, 128)
        norm = fold(rn * rn)
        suma = 0.5 * fold(pnew * pnew)
        sumb = 0.5 * fold(pnew * pold)
        xd[...] = xm[...] + beta * xd[...]
        for ranks in FWD_WAIT:
            modes(ranks)
        wait_sent(fsend, fs_sem)

        @pl.when(it == 0)
        def _():
            pltpu.make_async_copy(wf.at[pl.ds(0, 7)], wf.at[pl.ds(0, 7)], w2r).wait()

        for zz in range(8):
            cols = slice(256 * zz, 256 * zz + 256)
            xqn = xv_[:, cols] + beta * xq[:, cols]
            xq[:, cols] = xqn
            xn = xm[:, cols] - alpha * xqn
            xm[:, cols] = xn
            wx = wf[zz].astype(F32) * xn
            zb[:, cols] = wx.astype(BF16)
            qa, qc = wx * xn, wx * xd[:, cols]
            suma += fold(qa[:, :128] + qa[:, 128:])
            sumb += fold(qc[:, :128] + qc[:, 128:])
        row = lax.broadcasted_iota(jnp.int32, (8, 128), 0)
        one = [jnp.sum(part, axis=0, keepdims=True) for part in (norm, suma, sumb)]
        reduce_start(par, 0, jnp.where(row == 0, one[0], jnp.where(row == 1, one[1], one[2])))
        zv = zb[...]
        for a, b in BACK_SEND:
            w = dot(zv, tt[:, 64 * a:64 * b])
            for j in range((b - a) // 2):
                top, bottom = w[:16, 128 * j:128 * j + 128], w[16:, 128 * j:128 * j + 128]
                bsend[a + 2 * j] = jnp.where(left, top, swap(bottom)).astype(BF16)
                bsend[a + 2 * j + 1] = jnp.where(left, swap(top), bottom).astype(BF16)
            send_group((a, b), BACK_WAIT, bsend, brecv, bs_sem, br_sem)
        brecv[0] = bsend[0]
        yacc[...] = dot(gt[...], pb[...])

        @pl.when(it > 0)
        def _():
            shipped(osend, orecv.at[it - 1], or_sem.at[it - 1])
            advance(orecv.at[it - 1])

        part = reduce_finish(par, 0)
        reduce_start(par, 1, part)
        for ranks in BACK_WAIT:
            a, b = ranks
            wait_group(ranks, BACK_WAIT, brecv, br_sem)
            tiles = brecv[a:b].astype(F32)
            swapped = swap(tiles)
            vk[a:b, 0] = jnp.where(left, tiles, swapped).astype(BF16)
            vk[a:b, 1] = jnp.where(left, swapped, tiles).astype(BF16)
            part = yacc[...] + dot(sn[:, 32 * a:32 * b], vk[a:b].reshape(32 * (b - a), 128))
            if ranks != BACK_WAIT[-1]:
                yacc[...] = part
        wait_sent(bsend, bs_sem)
        ya = part.reshape(8, 2, 64, 128)
        vb[...] = ya.astype(BF16)
        im[...] = jnp.where(left, ya[:, 0], ya[:, 1])

    osend[...] = im[...].astype(BF16)
    ship(osend, olast, or_sem.at[ITERS - 1])
    scalars(ITERS - 1)
    alpha, beta = factors()
    xo_ref[...] = xb[...] + alpha * (rs[...] + beta * db[...])
    rs[...] = rs[...] - (alpha * beta) * qb[...]

    for o in range(3):
        sent(isend.at[0], i1s.at[o])
    for o in range(7):
        sent(i1.at[0], i2s.at[o])

    @pl.when(home)
    def _():
        for dx in range(1, 4):
            sent(pn.at[0, 0], psend_sem.at[dx - 1])
            sent(pw.at[0, 0], psend_sem.at[dx + 2])
    for o in range(1, 8):
        sent(w_cols.at[0], w1s.at[o - 1])
        sent(wf.at[0], w2s.at[o - 1])

    shipped(osend, olast, or_sem.at[ITERS - 1])
    for e in range(2):
        for h in range(2):
            a, b = olast[4 * e + 2 * h].astype(F32), olast[4 * e + 2 * h + 1].astype(F32)
            cols = slice(128 * h, 128 * h + 128)
            ro_ref[e, 0:64, cols] = rs[e, 0:64, cols] - alpha * jnp.where(left, a, swap(b))
            ro_ref[e, 64:128, cols] = rs[e, 64:128, cols] - alpha * jnp.where(left, swap(a), b)


def hand_over(x_in, r_in, x_out, r_out, x_held, r_held, sem):
    steps = ((x_in, x_held, x_out), (r_in, r_held, r_out))
    ins = [pltpu.make_async_copy(a, held, sem.at[n]) for n, (a, held, b) in enumerate(steps)]
    outs = [pltpu.make_async_copy(held, b, sem.at[2 + n]) for n, (a, held, b) in enumerate(steps)]
    for copy in ins:
        copy.start()
    for arrived, copy in zip(ins, outs):
        arrived.wait()
        copy.start()
    for copy in outs:
        copy.wait()


def per_device(right_side, spatial_basis, temporal_basis, spectral_weight, pierce_nodes, pierce_weights):
    vm = pltpu.VMEM
    dma = pltpu.SemaphoreType.DMA
    scratch = [
        vm((2, 128, 256), F32),
        vm((1024, 1024), BF16),
        vm((4, 256, 1024), BF16),
        vm((1024, 1024), BF16),
        vm((2048, 2048), BF16),
        vm((2048, 2048), BF16),
        vm((32, 1024), F32),
        vm((2, 2, 4, 512), jnp.int32),
        vm((2, 2, 4, 512), F32),
        vm((4, 512), jnp.int32),
        vm((4, 512), F32),
        vm((512, 1024), BF16),
        vm((1024, 512), BF16),
        vm((32, 32, 32), BF16),
        vm((4, 2, 64, 128), BF16),
        vm((8, 64, 128), BF16),
        vm((8, 64, 128), BF16),
        vm((8, 64, 128), F32),
        vm((8, 64, 128), F32),
        vm((8, 64, 128), F32),
        vm((8, 2, 64, 128), BF16),
        vm((32, 16, 128), BF16),
        vm((32, 16, 128), BF16),
        vm((32, 2048), BF16),
        vm((32, 2048), F32),
        vm((32, 2048), F32),
        vm((32, 2048), F32),
        vm((32, 2048), F32),
        vm((8, 32, 32), BF16),
        vm((8, 32, 256), BF16),
        vm((32, 2048), BF16),
        vm((32, 16, 128), BF16),
        vm((32, 16, 128), BF16),
        vm((32, 2, 16, 128), BF16),
        vm((512, 128), F32),
        vm((512, 128), F32),
        vm((512, 128), F32),
        vm((512, 128), F32),
        vm((512, 128), BF16),
        vm((1024, 128), F32),
        vm((2, 2, 16, 8, 128), F32),
        vm((4, 8, 128), F32),
        vm((2, 128, 256), F32),
        vm((2, 128, 256), F32),
        vm((2, 128, 256), F32),
        vm((8, 64, 128), BF16),
        vm((ITERS - 1, 8, 64, 128), BF16),
        vm((8, 64, 128), BF16),
        dma((6,)),
        dma((3,)),
        dma((3,)),
        dma((7,)),
        dma,
        dma((6,)),
        dma((2,)),
        dma((7,)),
        dma,
        dma((7,)),
        dma,
        dma,
        dma((4,)),
        dma,
        dma((4,)),
        dma((2, 2)),
        dma((2, 2)),
        dma((8,)),
        dma((ITERS,)),
    ]
    out = jax.ShapeDtypeStruct(right_side.shape, F32)
    results = pl.pallas_call(
        kernel,
        out_shape=(out, out),
        in_specs=[pl.BlockSpec(memory_space=pl.ANY)] * 6,
        out_specs=(pl.BlockSpec(memory_space=pltpu.VMEM),) * 2,
        scratch_shapes=scratch,
        name="cg",
        compiler_params=pltpu.CompilerParams(
            collective_id=0, has_side_effects=True, vmem_limit_bytes=56 * 2**20
        ),
    )(right_side, spatial_basis, temporal_basis, spectral_weight.T, pierce_nodes, pierce_weights)
    anywhere = (pl.BlockSpec(memory_space=pl.ANY),) * 2
    return pl.pallas_call(
        hand_over,
        out_shape=(out, out),
        in_specs=anywhere,
        out_specs=anywhere,
        scratch_shapes=[vm(right_side.shape, F32)] * 2 + [dma((4,))],
        compiler_params=pltpu.CompilerParams(vmem_limit_bytes=60 * 2**20),
        name="hand_over",
    )(*results)


def solution(mesh):
    placed = (
        P("dir", "space", "tm"),
        P(),
        P(),
        P(None, ("space", "tm")),
        P("dir", "tm", None, None),
        P("dir", "tm", None, None),
    )
    return jax.shard_map(
        per_device,
        mesh=mesh,
        in_specs=placed,
        out_specs=(P("dir", "space", "tm"), P("dir", "space", "tm")),
        check_vma=False,
    )
```
